512 devices in a mesh: page: 128 (over z, x, core), mp: 4 (over y).
Axes of the slice: x: 4, y: 4, z: 16, core: 2. Of those that a mesh axis runs over, the one named last changes fastest.
Arguments:
- queries: bfloat16 [2048, 8192], P('page', 'mp'), may hold values from -24 to 24
- cache_keys: bfloat16 [4096, 64, 1024], P('page', None, 'mp'), may hold values from -4 to 6
- cache_values: bfloat16 [4096, 64, 1024], P('page', None, 'mp'), may hold values from -6 to 6
- routes: int32 [2048, 8], P('page'), may hold values from 0 to 127, all different within a row; in each aligned block of 16 rows (0 to 15, 16 to 31, ...) at most 2 rows name the same one
- page_table: int32 [2048, 8, 2], P('page'), may hold values from 0 to 31
- lengths: int32 [2048], P('page'), may hold values from 897 to 1024
Outputs:
- attended: bfloat16 [2048, 8192], P('page', 'mp')
The draws below stay inside these ranges and needn't reach their ends.
Inputs may be any that keep to these rules, and one draw needn't show every extreme that they name: `routes`: each request names 8 different devices; among the 16 requests of one device no device is named more than 2 times, and some device exactly 2 times.
All inputs are finite; a program needn't handle non-finite values.
Results may differ from the reference program's by a relative error of at most 0.0055.
Values may be sent and summed in bfloat16 or wider, within the bound.
No kernel may reach another device: no remote copies, remote signals or barrier semaphores. Data moves between devices by JAX's collectives and lax.ppermute only.
A program may use at most 64 MiB of HBM per device.

```python
import math
import jax
import jax.numpy as jnp
import numpy as np
from jax import lax

QHEADS = 64
KVHEADS = 8
HEAD = 128
PAGE_LEN = 64
PPH = 2
HOPS = 8
PAGES_DEV = 32
REQ_DEV = 16
REQS = 2048
PAGES = 4096
SLOT = 2
N_PAGE = 128


def draw_queries(key, part):
    key = jax.random.fold_in(key, 11)
    base = jnp.clip(jax.random.normal(key, (REQS, QHEADS, HEAD), jnp.float32), -4.0, 4.0)
    return base.reshape(REQS, QHEADS * HEAD).astype(jnp.bfloat16)


def draw_cache_keys(key, part):
    key = jax.random.fold_in(key, 23)
    base = jnp.clip(jax.random.normal(key, (PAGES, PAGE_LEN, KVHEADS, HEAD), jnp.float32), -4.0, 4.0)
    return base.reshape(PAGES, PAGE_LEN, KVHEADS * HEAD).astype(jnp.bfloat16)


def with_ends(result, own_key, low, top_value):
    longest = result.shape.index(max(result.shape))
    spots = []
    for shift in (0, 1):
        where = [jax.random.randint(jax.random.fold_in(own_key, axis), (), 0, length) for axis, length in enumerate(result.shape)]
        where[longest] = (where[longest] + shift) % result.shape[longest]
        spots.append(tuple(where))
    return result.at[spots[0]].set(low).at[spots[1]].set(top_value)


def levels(rng, extent, split, smallest, largest):
    gain, own = 1.0, jax.random.fold_in(rng, 6)
    for dim, shards_of in split:
        draws = jnp.exp(jax.random.uniform(jax.random.fold_in(own, dim), (shards_of,), jnp.float32, smallest / len(split), largest / len(split)))
        gain = gain * jnp.repeat(draws, extent[dim] // shards_of).reshape([-1 if axis == dim else 1 for axis in range(len(extent))])
    return gain


def routed_block(own_key, own, number, rows, number_of, top, bound, skew):
    order = jax.random.permutation(own_key, number_of)
    crowded, ordinary = load_shares(number_of, rows * top, bound, skew, True), load_shares(number_of, rows * top, bound, skew, False)
    places = jnp.arange(number_of)

    def named(sizes, offset_by):
        used = int((sizes > 0).sum())
        fixed = max(1, used // 4)
        moved = fixed + (places - fixed + offset_by * (used - fixed)) % max(1, number_of - fixed)
        return jnp.zeros((number_of,), jnp.int32).at[order[jnp.where(places < fixed, places, moved)]].set(jnp.asarray(sizes, jnp.int32))

    sizes = jnp.where(number % 4 == 0, named(crowded, number // 4), named(ordinary, number - number // 4 - 1))
    mixed = jax.random.permutation(jax.random.fold_in(own, 3), number_of)
    giver, taker = mixed[0:number_of // 2 * 2:2], mixed[1:number_of // 2 * 2:2]
    margin = jnp.minimum(sizes[giver] - 1, bound - sizes[taker]) // 2
    margin = jnp.where((giver == order[0]) | (taker == order[0]) | (sizes[taker] == 0), 0, jnp.maximum(margin, 0))
    moved = jax.random.randint(jax.random.fold_in(own, 4), (number_of // 2,), 0, 1 << 20) % (margin + 1)
    sizes = sizes.at[giver].add(-moved).at[taker].add(moved)
    labels = jnp.searchsorted(jnp.cumsum(sizes), jnp.arange(rows * top), side="right").astype(jnp.int32)
    table = labels.reshape(top, rows).T
    table = table[jax.random.permutation(jax.random.fold_in(own, 1), rows)]
    offset_by = jax.random.randint(jax.random.fold_in(own, 2), (rows, 1), 0, top)
    return jnp.take_along_axis(table, (jnp.arange(top)[None, :] + offset_by) % top, axis=1)


def load_shares(count, total, reach, skew, full):
    loads = [(1 << 20) // math.isqrt(standing ** skew) + 1 for standing in range(1, count + 1)]
    largest = reach if full else min(reach, max(-(-total // count), total * loads[0] // sum(loads)))
    least = 1 if total - largest >= count - 1 else 0
    counts, rest = [largest] + [least] * (count - 1), total - largest - least * (count - 1)
    while rest > 0:
        candidates = [i for i in range(1, count) if counts[i] < largest] or [i for i in range(1, count) if counts[i] < reach]
        mass, budget = sum([loads[i] for i in candidates]), rest
        for i in candidates:
            more = min(reach - counts[i], max(1, budget * loads[i] // mass), rest)
            counts[i] = counts[i] + more
            rest = rest - more
    return np.array(counts)


def gaussian(own_key, extent, deviation, limit, cuts=(), kind=jnp.bfloat16):
    loudness = levels(own_key, extent, cuts, -0.22, 0.18) if cuts else 1.0
    values = jax.random.normal(own_key, extent, jnp.float32) * deviation * loudness
    return jnp.minimum(jnp.maximum(values, -limit), limit).astype(kind)


def setup_inputs(seed: int = 0) -> dict:
    splits = jax.random.split(jax.random.key(seed), 7)
    queries = draw_queries(jax.random.fold_in(splits[6], 71), 0)
    cache_keys = draw_cache_keys(jax.random.fold_in(splits[6], 71), 0)
    cache_values = gaussian(splits[2], (PAGES, PAGE_LEN, KVHEADS * HEAD), 1.0, 6.0, ((0, 128), (2, 4)))
    routes_keys = jax.random.split(jax.random.fold_in(splits[3], 1), REQS // REQ_DEV)
    routes_turns = jax.random.permutation(jax.random.fold_in(splits[3], 3), REQS // REQ_DEV)
    routes = jax.vmap(lambda own, number: routed_block(jax.random.fold_in(splits[3], 2), own, number, REQ_DEV, N_PAGE, HOPS, SLOT, 2))(routes_keys, routes_turns).reshape((REQS, HOPS))
    page_table = with_ends(jax.random.randint(splits[4], (REQS, HOPS, PPH), 0, PAGES_DEV), jax.random.fold_in(splits[4], 1), 0, PAGES_DEV - 1).astype(jnp.int32)
    lengths = with_ends(jax.random.randint(splits[5], (REQS,), (HOPS - 1) * PPH * PAGE_LEN + 1, HOPS * PPH * PAGE_LEN + 1), jax.random.fold_in(splits[5], 1), (HOPS - 1) * PPH * PAGE_LEN + 1, HOPS * PPH * PAGE_LEN).astype(jnp.int32)
    return dict(queries=queries, cache_keys=cache_keys, cache_values=cache_values, routes=routes, page_table=page_table, lengths=lengths)


def reference(queries, cache_keys, cache_values, routes, page_table, lengths):
    group = QHEADS // KVHEADS
    hop_tok = PPH * PAGE_LEN
    scale = HEAD ** -0.5

    def one_request(items):
        query_row, route_row, table_row, length = items
        pages = (route_row[:, None] * PAGES_DEV + table_row).reshape(-1).astype(jnp.int32)
        keys = cache_keys[pages].reshape(HOPS, hop_tok, KVHEADS, HEAD).astype(jnp.float32)
        values = cache_values[pages].reshape(HOPS, hop_tok, KVHEADS, HEAD).astype(jnp.float32)
        grouped = query_row.reshape(KVHEADS, group, HEAD).astype(jnp.float32)
        scores = jnp.einsum("kgd,htkd->hkgt", grouped, keys) * scale
        position = jnp.arange(HOPS, dtype=jnp.int32)[:, None] * hop_tok + jnp.arange(hop_tok, dtype=jnp.int32)[None, :]
        live = (position < length)[:, None, None, :]
        scores = jnp.where(live, scores, jnp.float32(-1e30))
        top = jnp.max(scores, axis=-1, keepdims=True)
        probs = jnp.exp(scores - top)
        total = jnp.sum(probs, axis=-1, keepdims=True)
        weights = lax.optimization_barrier(probs.astype(jnp.bfloat16)).astype(jnp.float32)
        partial_value = jnp.einsum("hkgt,htkd->hkgd", weights, values) / total
        partial_value = lax.optimization_barrier(partial_value.astype(jnp.bfloat16)).astype(jnp.float32)
        carry = top[..., 0] + jnp.log(total[..., 0])
        high = jnp.max(carry, axis=0, keepdims=True)
        share = jnp.exp(carry - high)
        merged = jnp.sum(share[..., None] * partial_value, axis=0) / jnp.sum(share, axis=0)[..., None]
        return merged.reshape(-1).astype(jnp.bfloat16)

    return lax.map(one_request, (queries, routes, page_table, lengths))
```

```python
import functools

import jax
import jax.numpy as jnp
from jax import lax
from jax.experimental import pallas as pl
from jax.experimental.pallas import tpu as pltpu
from jax.sharding import Mesh
from jax.sharding import PartitionSpec as P

HEAD = 128
HALVES = 4
SLOT = 2
DEAD = -1e30
EXTRA = 128
F32 = jnp.float32
BF16 = jnp.bfloat16


def iota(shape, dim):
    return lax.broadcasted_iota(jnp.int32, shape, dim)


def pieces(x):
    high = x.astype(BF16).astype(F32)
    mid = (x - high).astype(BF16).astype(F32)
    low = (x - high - mid).astype(BF16).astype(F32)
    return high, mid, low


def select_kernel(far, hops, base_ref, rows_ref, out_ref, sel_ref):
    count, width = rows_ref.shape
    width -= EXTRA
    cells = out_ref.shape[0]
    req_dev = count // far
    info = rows_ref[:, width:].astype(F32)
    lane = iota((count, cells), 1)
    row = iota((count, cells), 0)
    dest = (lane // (SLOT * far) + base_ref[0]).astype(F32)
    own = (lane // SLOT) % far == row // req_dev
    named = jnp.zeros((count, cells), F32)
    first = jnp.zeros((count, cells), F32)
    second = jnp.zeros((count, cells), F32)
    live = jnp.zeros((count, cells), F32)
    for hop in range(hops):
        hit = (info[:, hop : hop + 1] == dest) & own
        named = jnp.where(hit, 1.0, named)
        first = jnp.where(hit, info[:, hops + hop : hops + hop + 1], first)
        second = jnp.where(hit, info[:, 2 * hops + hop : 2 * hops + hop + 1], second)
        live = jnp.where(hit, info[:, 3 * hops + hop : 3 * hops + hop + 1], live)
    a = iota((count, count), 0)
    b = iota((count, count), 1)
    before = jnp.where((a // req_dev == b // req_dev) & (b < a), 1.0, 0.0).astype(BF16)
    rank = jnp.dot(before, named.astype(BF16), preferred_element_type=F32)
    sel = jnp.where(rank == (lane % SLOT).astype(F32), named, 0.0)
    sel_ref[...] = sel
    told = jnp.concatenate(
        [
            jnp.sum(sel * first, axis=0, keepdims=True),
            jnp.sum(sel * second, axis=0, keepdims=True),
            jnp.sum(sel * live, axis=0, keepdims=True),
            jnp.zeros((EXTRA - 3, cells), F32),
        ],
        axis=0,
    )
    out_ref[:, width:] = told.T.astype(BF16)
    place = jnp.concatenate([sel, jnp.zeros((128 - count, cells), F32)], axis=0).T.astype(BF16)
    queries = jnp.concatenate(
        [rows_ref[:, :width], jnp.zeros((128 - count, width), BF16)], axis=0
    )
    step = 256
    for col in range(0, width, step):
        out_ref[:, col : col + step] = jnp.dot(
            place, queries[:, col : col + step], preferred_element_type=F32
        ).astype(BF16)


def attend_kernel(
    rows_ref, keys_ref, values_ref, out_ref, told_ref, told_smem, q_ref, o_ref, carry_ref, sem
):
    cells, width = rows_ref.shape
    width -= EXTRA
    heads = width // HEAD
    group = heads // 2
    page_len, kv_width = keys_ref.shape[1], keys_ref.shape[2]
    hop_tok = 2 * page_len
    scale = HEAD ** -0.5
    told_ref[...] = rows_ref[:, width:].astype(F32).T[:8].astype(jnp.int32)
    copy = pltpu.make_async_copy(told_ref, told_smem, sem)
    copy.start()
    copy.wait()
    block = 16
    token = iota((heads, hop_tok), 1)
    lane = iota((heads, cells), 1)
    zero = jnp.zeros((group, HEAD), F32)

    def page(ref, which, cell):
        return ref[told_smem[which, cell]]

    def step(i, carries):
        start = pl.multiple_of(i * block, block)
        for head in range(heads):
            q_ref[head * block : (head + 1) * block, :] = rows_ref[
                pl.ds(start, block), head * HEAD : (head + 1) * HEAD
            ].astype(F32)
        for pair in range(0, block, 2):
            spread = []
            for cell in (pair, pair + 1):
                query = q_ref[pl.ds(cell, heads, stride=block), :]
                spread.append(jnp.concatenate([query[:group], zero], axis=1))
                spread.append(jnp.concatenate([zero, query[group:]], axis=1))
            spread = jnp.concatenate(spread, axis=0).astype(BF16)
            keys = jnp.concatenate(
                [page(keys_ref, which, start + cell) for cell in (pair, pair + 1) for which in (0, 1)],
                axis=0,
            )
            scores = lax.dot_general(
                spread, keys, (((1,), (1,)), ((), ())), preferred_element_type=F32
            ) * scale
            weights = []
            totals = []
            for n, cell in enumerate((pair, pair + 1)):
                own = scores[n * heads : (n + 1) * heads, n * hop_tok : (n + 1) * hop_tok]
                own = jnp.where(token < told_smem[2, start + cell], own, DEAD)
                top = jnp.max(own, axis=1, keepdims=True)
                probs = jnp.exp(own - top)
                total = jnp.sum(probs, axis=1, keepdims=True)
                carries = jnp.where(lane == start + cell, top + jnp.log(total), carries)
                nothing = jnp.zeros_like(probs)
                weights.append(
                    jnp.concatenate([probs, nothing] if n == 0 else [nothing, probs], axis=1)
                )
                totals.append(total)
            weights = jnp.concatenate(weights, axis=0).astype(BF16)
            values = jnp.concatenate(
                [page(values_ref, which, start + cell) for cell in (pair, pair + 1) for which in (0, 1)],
                axis=0,
            )
            mixed = jnp.dot(weights, values, preferred_element_type=F32)
            for n, cell in enumerate((pair, pair + 1)):
                at = n * heads
                o_ref[cell * heads : cell * heads + group, :] = (
                    mixed[at : at + group, :HEAD] / totals[n][:group]
                )
                o_ref[cell * heads + group : (cell + 1) * heads, :] = (
                    mixed[at + group : at + heads, HEAD:] / totals[n][group:]
                )
        for head in range(heads):
            out_ref[pl.ds(start, block), head * HEAD : (head + 1) * HEAD] = o_ref[
                pl.ds(head, block, stride=heads), :
            ].astype(BF16)
        return carries

    carries = lax.fori_loop(0, cells // block, step, jnp.zeros((heads, cells), F32))
    parts = pieces(carries)
    told = jnp.concatenate(
        [*parts, jnp.zeros((EXTRA - 3 * heads, cells), F32)], axis=0
    )
    out_ref[:, width:] = told.T.astype(BF16)


def merge_kernel(last, rows_ref, sel_ref, out_ref):
    cells, width = rows_ref.shape
    width -= EXTRA
    heads = width // HEAD
    count = sel_ref.shape[0]
    chosen = sel_ref[...] > 0.0
    info = rows_ref[:, width:].astype(F32)
    if cells < 128:
        info = jnp.concatenate([info, jnp.zeros((128 - cells, EXTRA), F32)], axis=0)
    info = info.T
    carries = (info[:heads] + info[heads : 2 * heads] + info[2 * heads : 3 * heads])[:, :cells]
    lane = iota((count, EXTRA), 1)
    told = jnp.zeros((count, EXTRA), F32)
    for head in range(heads):
        carry = jnp.broadcast_to(carries[head : head + 1], (count, cells))
        high = jnp.max(jnp.where(chosen, carry, DEAD), axis=1, keepdims=True)
        share = jnp.where(chosen, jnp.exp(jnp.minimum(carry - high, 0.0)), 0.0)
        total = jnp.sum(share, axis=1, keepdims=True)
        some = total > 0.0
        share = share / jnp.where(some, total, 1.0)
        major = share.astype(BF16)
        minor = (share - major.astype(F32)).astype(BF16)
        both = jnp.dot(
            jnp.concatenate([major, minor], axis=0),
            rows_ref[:, head * HEAD : (head + 1) * HEAD],
            preferred_element_type=F32,
        )
        out_ref[:, head * HEAD : (head + 1) * HEAD] = (both[:count] + both[count:]).astype(BF16)
        if not last:
            carry = jnp.where(some, high + jnp.log(jnp.where(some, total, 1.0)), DEAD)
            for n, part in enumerate(pieces(carry)):
                told = jnp.where(lane == n * heads + head, part, told)
    if not last:
        out_ref[:, width:] = told.astype(BF16)


def per_device(queries, cache_keys, cache_values, routes, page_table, lengths):
    far = lax.axis_size("far")
    near = lax.axis_size("near")
    req_dev, hops = routes.shape
    width = queries.shape[1]
    heads = width // HEAD
    hop_tok = page_table.shape[2] * cache_keys.shape[1]
    cells = near * far * SLOT
    count = far * req_dev
    full = width + EXTRA
    vmem = pl.BlockSpec(memory_space=pltpu.VMEM)
    params = pltpu.CompilerParams(vmem_limit_bytes=48 * 1024 * 1024)

    live_hop = jnp.clip(
        lengths[:, None] - jnp.arange(hops, dtype=jnp.int32)[None, :] * hop_tok, 0, hop_tok
    )
    info = jnp.concatenate([routes, page_table[:, :, 0], page_table[:, :, 1], live_hop], axis=1)
    info = jnp.pad(info, ((0, 0), (0, EXTRA - info.shape[1]))).astype(BF16)
    rows = jnp.concatenate([queries, info], axis=1)
    if far > 1:
        rows = jnp.broadcast_to(rows[None], (far, req_dev, full))
        rows = lax.all_to_all(rows, "far", split_axis=0, concat_axis=0, tiled=True)
        rows = rows.reshape(count, full)
    base = (lax.axis_index("far") * near).astype(jnp.int32).reshape(1)
    cell_rows, sel = pl.pallas_call(
        functools.partial(select_kernel, far, hops),
        out_shape=(
            jax.ShapeDtypeStruct((cells, full), BF16),
            jax.ShapeDtypeStruct((count, cells), F32),
        ),
        in_specs=[pl.BlockSpec(memory_space=pltpu.SMEM), vmem],
        out_specs=(vmem, vmem),
        compiler_params=params,
        name="select",
    )(base, rows)
    cell_rows = lax.all_to_all(
        cell_rows.reshape(near, far * SLOT, full), "near", split_axis=0, concat_axis=0, tiled=True
    ).reshape(cells, full)
    partial = pl.pallas_call(
        attend_kernel,
        out_shape=jax.ShapeDtypeStruct((cells, full), BF16),
        in_specs=[vmem] * 3,
        out_specs=vmem,
        scratch_shapes=[
            pltpu.VMEM((8, cells), jnp.int32),
            pltpu.SMEM((8, cells), jnp.int32),
            pltpu.VMEM((16 * heads, HEAD), F32),
            pltpu.VMEM((16 * heads, HEAD), F32),
            pltpu.VMEM((heads, cells), F32),
            pltpu.SemaphoreType.DMA,
        ],
        compiler_params=params,
        name="attend",
    )(cell_rows, cache_keys, cache_values)
    partial = lax.all_to_all(
        partial.reshape(near, far * SLOT, full), "near", split_axis=0, concat_axis=0, tiled=True
    ).reshape(cells, full)
    if far > 1:
        partial = pl.pallas_call(
            functools.partial(merge_kernel, False),
            out_shape=jax.ShapeDtypeStruct((count, full), BF16),
            in_specs=[vmem] * 2,
            out_specs=vmem,
            compiler_params=params,
            name="merge_near",
        )(partial, sel)
        partial = lax.all_to_all(
            partial.reshape(far, req_dev, full), "far", split_axis=0, concat_axis=0, tiled=True
        ).reshape(count, full)
        sel = (
            jnp.arange(count, dtype=jnp.int32)[None, :] % req_dev
            == jnp.arange(req_dev, dtype=jnp.int32)[:, None]
        ).astype(F32)
    return pl.pallas_call(
        functools.partial(merge_kernel, True),
        out_shape=jax.ShapeDtypeStruct((req_dev, width), BF16),
        in_specs=[vmem] * 2,
        out_specs=vmem,
        compiler_params=params,
        name="merge_far",
    )(partial, sel)


def solution(mesh):
    pages, heads = mesh.devices.shape
    fine = Mesh(mesh.devices.reshape(HALVES, pages // HALVES, heads), ("far", "near", "mp"))
    page = ("far", "near")
    placed = (
        P(page, "mp"),
        P(page, None, "mp"),
        P(page, None, "mp"),
        P(page, None),
        P(page, None, None),
        P(page),
    )
    return jax.shard_map(
        per_device, mesh=fine, in_specs=placed, out_specs=P(page, "mp"), check_vma=False
    )
```

```python
import functools

import jax
import jax.numpy as jnp
from jax import lax
from jax.experimental import pallas as pl
from jax.experimental.pallas import tpu as pltpu
from jax.sharding import PartitionSpec as P

HEAD = 128
FAR = 4
SLOT = 2
BLOCK = 16
DEAD = -1e30
EXTRA = 128
F32 = jnp.float32
BF16 = jnp.bfloat16


def iota(shape, dim):
    return lax.broadcasted_iota(jnp.int32, shape, dim)


def pieces(x):
    high = x.astype(BF16).astype(F32)
    mid = (x - high).astype(BF16).astype(F32)
    low = (x - high - mid).astype(BF16).astype(F32)
    return high, mid, low


def pack_kernel(hop_tok, queries_ref, routes_ref, tables_ref, lengths_ref, out_ref):
    far, req_dev, width = out_ref.shape
    width -= EXTRA
    hops = routes_ref.shape[0]
    live = jnp.clip(lengths_ref[...] - iota((hops, req_dev), 0) * hop_tok, 0, hop_tok)
    told = jnp.concatenate([routes_ref[...], live, tables_ref[...]], axis=0).astype(F32)
    told = jnp.concatenate([told, jnp.zeros((told.shape[0], 128 - req_dev), F32)], axis=1)
    told = jnp.concatenate([told, jnp.zeros((EXTRA - told.shape[0], 128), F32)], axis=0)
    told = told.T[:req_dev].astype(BF16)
    for n in range(far):
        out_ref[n, :, :width] = queries_ref[...]
        out_ref[n, :, width:] = told


def select_kernel(far, hops, base_ref, rows_ref, out_ref, sel_ref):
    count, width = rows_ref.shape
    width -= EXTRA
    cells = out_ref.shape[0]
    req_dev = count // far
    info = rows_ref[:, width:].astype(F32)
    lane = iota((count, cells), 1)
    row = iota((count, cells), 0)
    dest = (lane // (SLOT * far) + base_ref[0]).astype(F32)
    own = (lane // SLOT) % far == row // req_dev
    named = jnp.zeros((count, cells), F32)
    first = jnp.zeros((count, cells), F32)
    second = jnp.zeros((count, cells), F32)
    live = jnp.zeros((count, cells), F32)
    for hop in range(hops):
        hit = (info[:, hop : hop + 1] == dest) & own
        named = jnp.where(hit, 1.0, named)
        live = jnp.where(hit, info[:, hops + hop : hops + hop + 1], live)
        at = 2 * hops + 2 * hop
        first = jnp.where(hit, info[:, at : at + 1], first)
        second = jnp.where(hit, info[:, at + 1 : at + 2], second)
    a = iota((count, count), 0)
    b = iota((count, count), 1)
    before = jnp.where((a // req_dev == b // req_dev) & (b < a), 1.0, 0.0).astype(BF16)
    rank = jnp.dot(before, named.astype(BF16), preferred_element_type=F32)
    sel = jnp.where(rank == (lane % SLOT).astype(F32), named, 0.0)
    sel_ref[...] = sel
    told = jnp.concatenate(
        [
            jnp.sum(sel * first, axis=0, keepdims=True),
            jnp.sum(sel * second, axis=0, keepdims=True),
            jnp.sum(sel * live, axis=0, keepdims=True),
            jnp.zeros((EXTRA - 3, cells), F32),
        ],
        axis=0,
    )
    out_ref[:, width:] = told.T.astype(BF16)
    place = jnp.concatenate([sel, jnp.zeros((128 - count, cells), F32)], axis=0).T.astype(BF16)
    queries = jnp.concatenate(
        [rows_ref[:, :width], jnp.zeros((128 - count, width), BF16)], axis=0
    )
    step = 256
    for col in range(0, width, step):
        out_ref[:, col : col + step] = jnp.dot(
            place, queries[:, col : col + step], preferred_element_type=F32
        ).astype(BF16)


def attend_kernel(
    rows_ref,
    keys_ref,
    values_ref,
    out_ref,
    told_ref,
    told_smem,
    query_ref,
    score_ref,
    prob_ref,
    inverse_ref,
    mixed_ref,
    sem,
):
    cells, width = rows_ref.shape
    width -= EXTRA
    heads = width // HEAD
    group = heads // 2
    hop_tok = 2 * keys_ref.shape[1]
    scale = HEAD ** -0.5
    told_ref[...] = rows_ref[:, width:].astype(F32).T[:8].astype(jnp.int32)
    copy = pltpu.make_async_copy(told_ref, told_smem, sem)
    copy.start()
    copy.wait()
    block = BLOCK
    blocks = cells // block
    token = iota((heads, hop_tok), 1)
    lane = iota((heads, cells), 1)
    zero = jnp.zeros((group, HEAD), F32)
    nothing = jnp.zeros((heads, hop_tok), BF16)

    def pages(ref, cell):
        return jnp.concatenate(
            [ref[told_smem[which, cell + n]] for n in (0, 1) for which in (0, 1)], axis=0
        )

    def scores(i):
        start = pl.multiple_of(i * block, block)
        for head in range(heads):
            query_ref[head * block : (head + 1) * block, :] = rows_ref[
                pl.ds(start, block), head * HEAD : (head + 1) * HEAD
            ].astype(F32)
        for pair in range(0, block, 2):
            spread = []
            for cell in (pair, pair + 1):
                query = query_ref[pl.ds(cell, heads, stride=block), :]
                spread.append(jnp.concatenate([query[:group], zero], axis=1))
                spread.append(jnp.concatenate([zero, query[group:]], axis=1))
            both = lax.dot_general(
                jnp.concatenate(spread, axis=0).astype(BF16),
                pages(keys_ref, start + pair),
                (((1,), (1,)), ((), ())),
                preferred_element_type=F32,
            )
            at = pl.multiple_of((start + pair) * heads, 2 * heads)
            score_ref[pl.ds(at, heads), :] = both[:heads, :hop_tok]
            score_ref[pl.ds(at + heads, heads), :] = both[heads:, hop_tok:]

    def softmax(i, carries):
        start = pl.multiple_of(i * block, block)
        for cell in range(block):
            at = pl.multiple_of((start + cell) * heads, heads)
            own = score_ref[pl.ds(at, heads), :] * scale
            own = jnp.where(token < told_smem[2, start + cell], own, DEAD)
            top = jnp.max(own, axis=1, keepdims=True)
            probs = jnp.exp(own - top)
            total = jnp.sum(probs, axis=1, keepdims=True)
            carries = jnp.where(lane == start + cell, top + jnp.log(total), carries)
            prob_ref[pl.ds(at, heads), :] = probs.astype(BF16)
            inverse_ref[pl.ds(at, heads), :] = jnp.broadcast_to(1.0 / total, (heads, HEAD))
        return carries

    def mix(i):
        start = pl.multiple_of(i * block, block)
        for pair in range(0, block, 2):
            at = pl.multiple_of((start + pair) * heads, 2 * heads)
            one = jnp.concatenate([prob_ref[pl.ds(at, heads), :], nothing], axis=1)
            two = jnp.concatenate([nothing, prob_ref[pl.ds(at + heads, heads), :]], axis=1)
            both = jnp.dot(
                jnp.concatenate([one, two], axis=0),
                pages(values_ref, start + pair),
                preferred_element_type=F32,
            )
            inverse = inverse_ref[pl.ds(at, 2 * heads), :]
            for n in (0, 1):
                low, mid, high = n * heads, n * heads + group, (n + 1) * heads
                to = pair * heads
                mixed_ref[to + low : to + mid, :] = both[low:mid, :HEAD] * inverse[low:mid]
                mixed_ref[to + mid : to + high, :] = both[mid:high, HEAD:] * inverse[mid:high]
        for head in range(heads):
            out_ref[pl.ds(start, block), head * HEAD : (head + 1) * HEAD] = mixed_ref[
                pl.ds(head, block, stride=heads), :
            ].astype(BF16)

    def step(i, carries):
        mix(jnp.maximum(i - 2, 0))
        carries = softmax(jnp.clip(i - 1, 0, blocks - 1), carries)
        scores(jnp.minimum(i, blocks - 1))
        return carries

    carries = lax.fori_loop(0, blocks + 2, step, jnp.zeros((heads, cells), F32))
    told = jnp.concatenate(
        [*pieces(carries), jnp.zeros((EXTRA - 3 * heads, cells), F32)], axis=0
    )
    out_ref[:, width:] = told.T.astype(BF16)


def merge_kernel(last, rows_ref, sel_ref, out_ref):
    cells, width = rows_ref.shape
    width -= EXTRA
    heads = width // HEAD
    count = sel_ref.shape[0]
    chosen = sel_ref[...] > 0.0
    info = rows_ref[:, width:].astype(F32)
    if cells < 128:
        info = jnp.concatenate([info, jnp.zeros((128 - cells, EXTRA), F32)], axis=0)
    info = info.T
    carries = (info[:heads] + info[heads : 2 * heads] + info[2 * heads : 3 * heads])[:, :cells]
    lane = iota((count, EXTRA), 1)
    told = jnp.zeros((count, EXTRA), F32)
    for head in range(heads):
        carry = jnp.broadcast_to(carries[head : head + 1], (count, cells))
        high = jnp.max(jnp.where(chosen, carry, DEAD), axis=1, keepdims=True)
        share = jnp.where(chosen, jnp.exp(jnp.minimum(carry - high, 0.0)), 0.0)
        total = jnp.sum(share, axis=1, keepdims=True)
        some = total > 0.0
        share = share / jnp.where(some, total, 1.0)
        major = share.astype(BF16)
        minor = (share - major.astype(F32)).astype(BF16)
        both = jnp.dot(
            jnp.concatenate([major, minor], axis=0),
            rows_ref[:, head * HEAD : (head + 1) * HEAD],
            preferred_element_type=F32,
        )
        out_ref[:, head * HEAD : (head + 1) * HEAD] = (both[:count] + both[count:]).astype(BF16)
        if not last:
            carry = jnp.where(some, high + jnp.log(jnp.where(some, total, 1.0)), DEAD)
            for n, part in enumerate(pieces(carry)):
                told = jnp.where(lane == n * heads + head, part, told)
    if not last:
        out_ref[:, width:] = told.astype(BF16)


def far_sets(far, near):
    quarter = near // 4
    turn = [[m ^ quarter if n >= far // 2 else m for m in range(near)] for n in range(far)]
    return [[n * near + turn[n][m] for n in range(far)] for m in range(near)]


def per_device(queries, cache_keys, cache_values, routes, page_table, lengths):
    pages = lax.axis_size("page")
    far, near = FAR, pages // FAR
    near_groups = [[n * near + m for m in range(near)] for n in range(far)]
    far_groups = far_sets(far, near)
    req_dev, hops = routes.shape
    width = queries.shape[1]
    heads = width // HEAD
    hop_tok = page_table.shape[2] * cache_keys.shape[1]
    cells = near * far * SLOT
    count = far * req_dev
    full = width + EXTRA
    vmem = pl.BlockSpec(memory_space=pltpu.VMEM)
    params = pltpu.CompilerParams(vmem_limit_bytes=48 * 1024 * 1024)

    rows = pl.pallas_call(
        functools.partial(pack_kernel, hop_tok),
        out_shape=jax.ShapeDtypeStruct((far, req_dev, full), BF16),
        in_specs=[vmem] * 4,
        out_specs=vmem,
        compiler_params=params,
        name="pack",
    )(
        queries,
        routes.T,
        page_table.transpose(1, 2, 0).reshape(-1, req_dev),
        lengths.reshape(1, req_dev),
    )
    if far > 1:
        rows = lax.all_to_all(
            rows, "page", split_axis=0, concat_axis=0, axis_index_groups=far_groups, tiled=True
        )
    rows = rows.reshape(count, full)
    base = (lax.axis_index("page") // near * near).astype(jnp.int32).reshape(1)
    cell_rows, sel = pl.pallas_call(
        functools.partial(select_kernel, far, hops),
        out_shape=(
            jax.ShapeDtypeStruct((cells, full), BF16),
            jax.ShapeDtypeStruct((count, cells), F32),
        ),
        in_specs=[pl.BlockSpec(memory_space=pltpu.SMEM), vmem],
        out_specs=(vmem, vmem),
        compiler_params=params,
        name="select",
    )(base, rows)
    cell_rows = lax.all_to_all(
        cell_rows.reshape(near, far * SLOT, full), "page", split_axis=0, concat_axis=0,
        axis_index_groups=near_groups, tiled=True,
    ).reshape(cells, full)
    partial = pl.pallas_call(
        attend_kernel,
        out_shape=jax.ShapeDtypeStruct((cells, full), BF16),
        in_specs=[vmem] * 3,
        out_specs=vmem,
        scratch_shapes=[
            pltpu.VMEM((8, cells), jnp.int32),
            pltpu.SMEM((8, cells), jnp.int32),
            pltpu.VMEM((BLOCK * heads, HEAD), F32),
            pltpu.VMEM((cells * heads, HEAD), F32),
            pltpu.VMEM((cells * heads, HEAD), BF16),
            pltpu.VMEM((cells * heads, HEAD), F32),
            pltpu.VMEM((BLOCK * heads, HEAD), F32),
            pltpu.SemaphoreType.DMA,
        ],
        compiler_params=params,
        name="attend",
    )(cell_rows, cache_keys, cache_values)
    partial = lax.all_to_all(
        partial.reshape(near, far * SLOT, full), "page", split_axis=0, concat_axis=0,
        axis_index_groups=near_groups, tiled=True,
    ).reshape(cells, full)
    if far > 1:
        partial = pl.pallas_call(
            functools.partial(merge_kernel, False),
            out_shape=jax.ShapeDtypeStruct((count, full), BF16),
            in_specs=[vmem] * 2,
            out_specs=vmem,
            compiler_params=params,
            name="merge_near",
        )(partial, sel)
        partial = lax.all_to_all(
            partial.reshape(far, req_dev, full), "page", split_axis=0, concat_axis=0,
            axis_index_groups=far_groups, tiled=True,
        ).reshape(count, full)
        sel = (
            jnp.arange(count, dtype=jnp.int32)[None, :] % req_dev
            == jnp.arange(req_dev, dtype=jnp.int32)[:, None]
        ).astype(F32)
    return pl.pallas_call(
        functools.partial(merge_kernel, True),
        out_shape=jax.ShapeDtypeStruct((req_dev, width), BF16),
        in_specs=[vmem] * 2,
        out_specs=vmem,
        compiler_params=params,
        name="merge_far",
    )(partial, sel)


def solution(mesh):
    placed = (
        P("page", "mp"),
        P("page", None, "mp"),
        P("page", None, "mp"),
        P("page", None),
        P("page", None, None),
        P("page"),
    )
    return jax.shard_map(
        per_device, mesh=mesh, in_specs=placed, out_specs=P("page", "mp"), check_vma=False
    )
```

```python
import functools

import jax
import jax.numpy as jnp
from jax import lax
from jax.experimental import pallas as pl
from jax.experimental.pallas import tpu as pltpu
from jax.sharding import PartitionSpec as P

HEAD = 128
FAR = 8
PLANE = 8
SLOT = 2
BLOCK = 16
DEAD = -1e30
EXTRA = 128
F32 = jnp.float32
BF16 = jnp.bfloat16


def iota(shape, dim):
    return lax.broadcasted_iota(jnp.int32, shape, dim)


def pieces(x):
    high = x.astype(BF16).astype(F32)
    mid = (x - high).astype(BF16).astype(F32)
    low = (x - high - mid).astype(BF16).astype(F32)
    return high, mid, low


def pack_kernel(
    hop_tok, queries_in, routes_in, tables_in, lengths_in, out_ref,
    queries_ref, routes_ref, tables_ref, lengths_ref, sems,
):
    far, req_dev, width = out_ref.shape
    width -= EXTRA
    copies = [
        pltpu.make_async_copy(a, b, sems.at[n])
        for n, (a, b) in enumerate(
            [
                (queries_in, queries_ref),
                (routes_in, routes_ref),
                (tables_in, tables_ref),
                (lengths_in, lengths_ref),
            ]
        )
    ]
    for copy in copies:
        copy.start()
    for copy in copies:
        copy.wait()
    hops = routes_ref.shape[0]
    live = jnp.clip(lengths_ref[...] - iota((hops, req_dev), 0) * hop_tok, 0, hop_tok)
    told = jnp.concatenate([routes_ref[...], live, tables_ref[...]], axis=0).astype(F32)
    told = jnp.concatenate([told, jnp.zeros((told.shape[0], 128 - req_dev), F32)], axis=1)
    told = jnp.concatenate([told, jnp.zeros((EXTRA - told.shape[0], 128), F32)], axis=0)
    told = told.T[:req_dev].astype(BF16)
    for n in range(far):
        out_ref[n, :, :width] = queries_ref[...]
        out_ref[n, :, width:] = told


def select_kernel(far, hops, base_ref, rows_ref, out_ref, sel_ref):
    count, width = rows_ref.shape
    width -= EXTRA
    cells = out_ref.shape[0]
    req_dev = count // far
    info = rows_ref[:, width:].astype(F32)
    lane = iota((count, cells), 1)
    row = iota((count, cells), 0)
    dest = (lane // (SLOT * far) + base_ref[0]).astype(F32)
    own = (lane // SLOT) % far == row // req_dev
    named = jnp.zeros((count, cells), F32)
    first = jnp.zeros((count, cells), F32)
    second = jnp.zeros((count, cells), F32)
    live = jnp.zeros((count, cells), F32)
    for hop in range(hops):
        hit = (info[:, hop : hop + 1] == dest) & own
        named = jnp.where(hit, 1.0, named)
        live = jnp.where(hit, info[:, hops + hop : hops + hop + 1], live)
        at = 2 * hops + 2 * hop
        first = jnp.where(hit, info[:, at : at + 1], first)
        second = jnp.where(hit, info[:, at + 1 : at + 2], second)
    a = iota((count, count), 0)
    b = iota((count, count), 1)
    before = jnp.where((a // req_dev == b // req_dev) & (b < a), 1.0, 0.0).astype(BF16)
    rank = jnp.dot(before, named.astype(BF16), preferred_element_type=F32)
    sel = jnp.where(rank == (lane % SLOT).astype(F32), named, 0.0)
    sel_ref[...] = sel
    told = jnp.concatenate(
        [
            jnp.sum(sel * first, axis=0, keepdims=True),
            jnp.sum(sel * second, axis=0, keepdims=True),
            jnp.sum(sel * live, axis=0, keepdims=True),
            jnp.zeros((EXTRA - 3, cells), F32),
        ],
        axis=0,
    )
    out_ref[:, width:] = told.T.astype(BF16)
    place = sel.T.astype(BF16)
    step = 256
    for col in range(0, width, step):
        out_ref[:, col : col + step] = jnp.dot(
            place, rows_ref[:, col : col + step], preferred_element_type=F32
        ).astype(BF16)


def attend_kernel(
    rows_ref,
    keys_ref,
    values_ref,
    out_ref,
    told_ref,
    told_smem,
    query_ref,
    score_ref,
    prob_ref,
    inverse_ref,
    mixed_ref,
    sem,
):
    cells, width = rows_ref.shape
    width -= EXTRA
    heads = width // HEAD
    group = heads // 2
    hop_tok = 2 * keys_ref.shape[1]
    scale = HEAD ** -0.5
    told_ref[...] = rows_ref[:, width:].astype(F32).T[:8].astype(jnp.int32)
    copy = pltpu.make_async_copy(told_ref, told_smem, sem)
    copy.start()
    copy.wait()
    block = BLOCK
    blocks = cells // block
    token = iota((heads, hop_tok), 1)
    lane = iota((heads, cells), 1)
    zero = jnp.zeros((group, HEAD), F32)
    nothing = jnp.zeros((heads, hop_tok), BF16)

    def pages(ref, cell):
        return jnp.concatenate(
            [ref[told_smem[which, cell + n]] for n in (0, 1) for which in (0, 1)], axis=0
        )

    def scores(i):
        start = pl.multiple_of(i * block, block)
        for head in range(heads):
            query_ref[head * block : (head + 1) * block, :] = rows_ref[
                pl.ds(start, block), head * HEAD : (head + 1) * HEAD
            ].astype(F32)
        for pair in range(0, block, 2):
            spread = []
            for cell in (pair, pair + 1):
                query = query_ref[pl.ds(cell, heads, stride=block), :]
                spread.append(jnp.concatenate([query[:group], zero], axis=1))
                spread.append(jnp.concatenate([zero, query[group:]], axis=1))
            both = lax.dot_general(
                jnp.concatenate(spread, axis=0).astype(BF16),
                pages(keys_ref, start + pair),
                (((1,), (1,)), ((), ())),
                preferred_element_type=F32,
            )
            at = pl.multiple_of((start + pair) * heads, 2 * heads)
            score_ref[pl.ds(at, heads), :] = both[:heads, :hop_tok]
            score_ref[pl.ds(at + heads, heads), :] = both[heads:, hop_tok:]

    def softmax(i, carries):
        start = pl.multiple_of(i * block, block)
        for cell in range(block):
            at = pl.multiple_of((start + cell) * heads, heads)
            own = score_ref[pl.ds(at, heads), :] * scale
            own = jnp.where(token < told_smem[2, start + cell], own, DEAD)
            top = jnp.max(own, axis=1, keepdims=True)
            probs = jnp.exp(own - top)
            total = jnp.sum(probs, axis=1, keepdims=True)
            carries = jnp.where(lane == start + cell, top + jnp.log(total), carries)
            prob_ref[pl.ds(at, heads), :] = probs.astype(BF16)
            inverse_ref[pl.ds(at, heads), :] = jnp.broadcast_to(1.0 / total, (heads, HEAD))
        return carries

    def mix(i):
        start = pl.multiple_of(i * block, block)
        for pair in range(0, block, 2):
            at = pl.multiple_of((start + pair) * heads, 2 * heads)
            one = jnp.concatenate([prob_ref[pl.ds(at, heads), :], nothing], axis=1)
            two = jnp.concatenate([nothing, prob_ref[pl.ds(at + heads, heads), :]], axis=1)
            both = jnp.dot(
                jnp.concatenate([one, two], axis=0),
                pages(values_ref, start + pair),
                preferred_element_type=F32,
            )
            inverse = inverse_ref[pl.ds(at, 2 * heads), :]
            for n in (0, 1):
                low, mid, high = n * heads, n * heads + group, (n + 1) * heads
                to = pair * heads
                mixed_ref[to + low : to + mid, :] = both[low:mid, :HEAD] * inverse[low:mid]
                mixed_ref[to + mid : to + high, :] = both[mid:high, HEAD:] * inverse[mid:high]
        for head in range(heads):
            out_ref[pl.ds(start, block), head * HEAD : (head + 1) * HEAD] = mixed_ref[
                pl.ds(head, block, stride=heads), :
            ].astype(BF16)

    def step(i, carries):
        mix(jnp.maximum(i - 2, 0))
        carries = softmax(jnp.clip(i - 1, 0, blocks - 1), carries)
        scores(jnp.minimum(i, blocks - 1))
        return carries

    carries = lax.fori_loop(0, blocks + 2, step, jnp.zeros((heads, cells), F32))
    told = jnp.concatenate(
        [*pieces(carries), jnp.zeros((EXTRA - 3 * heads, cells), F32)], axis=0
    )
    out_ref[:, width:] = told.T.astype(BF16)


def merge_kernel(last, rows_ref, sel_ref, out_ref):
    cells, width = rows_ref.shape
    width -= EXTRA
    heads = width // HEAD
    count = sel_ref.shape[0]
    chosen = sel_ref[...] > 0.0
    info = rows_ref[:, width:].astype(F32)
    if cells < 128:
        info = jnp.concatenate([info, jnp.zeros((128 - cells, EXTRA), F32)], axis=0)
    info = info.T
    carries = (info[:heads] + info[heads : 2 * heads] + info[2 * heads : 3 * heads])[:, :cells]
    lane = iota((count, EXTRA), 1)
    told = jnp.zeros((count, EXTRA), F32)
    for head in range(heads):
        carry = jnp.broadcast_to(carries[head : head + 1], (count, cells))
        high = jnp.max(jnp.where(chosen, carry, DEAD), axis=1, keepdims=True)
        share = jnp.where(chosen, jnp.exp(jnp.minimum(carry - high, 0.0)), 0.0)
        total = jnp.sum(share, axis=1, keepdims=True)
        some = total > 0.0
        share = share / jnp.where(some, total, 1.0)
        major = share.astype(BF16)
        minor = (share - major.astype(F32)).astype(BF16)
        both = jnp.dot(
            jnp.concatenate([major, minor], axis=0),
            rows_ref[:, head * HEAD : (head + 1) * HEAD],
            preferred_element_type=F32,
        )
        out_ref[:, head * HEAD : (head + 1) * HEAD] = (both[:count] + both[count:]).astype(BF16)
        if not last:
            carry = jnp.where(some, high + jnp.log(jnp.where(some, total, 1.0)), DEAD)
            for n, part in enumerate(pieces(carry)):
                told = jnp.where(lane == n * heads + head, part, told)
    if not last:
        out_ref[:, width:] = told.astype(BF16)


def far_sets(far, near):
    turn = [[m ^ PLANE if n >= far // 2 else m for m in range(near)] for n in range(far)]
    return [[n * near + turn[n][m] for n in range(far)] for m in range(near)]


def per_device(queries, cache_keys, cache_values, routes, page_table, lengths):
    pages = lax.axis_size("page")
    far, near = FAR, pages // FAR
    near_groups = [[n * near + m for m in range(near)] for n in range(far)]
    far_groups = far_sets(far, near)
    req_dev, hops = routes.shape
    width = queries.shape[1]
    heads = width // HEAD
    hop_tok = page_table.shape[2] * cache_keys.shape[1]
    cells = near * far * SLOT
    count = far * req_dev
    full = width + EXTRA
    vmem = pl.BlockSpec(memory_space=pltpu.VMEM)
    params = pltpu.CompilerParams(vmem_limit_bytes=48 * 1024 * 1024)

    rows = pl.pallas_call(
        functools.partial(pack_kernel, hop_tok),
        out_shape=jax.ShapeDtypeStruct((far, req_dev, full), BF16),
        in_specs=[pl.BlockSpec(memory_space=pl.ANY)] * 4,
        out_specs=vmem,
        scratch_shapes=[
            pltpu.VMEM((req_dev, width), BF16),
            pltpu.VMEM((hops, req_dev), jnp.int32),
            pltpu.VMEM((hops * page_table.shape[2], req_dev), jnp.int32),
            pltpu.VMEM((1, req_dev), jnp.int32),
            pltpu.SemaphoreType.DMA((4,)),
        ],
        compiler_params=pltpu.CompilerParams(vmem_limit_bytes=60 * 1024 * 1024),
        name="pack",
    )(
        queries,
        routes.T,
        page_table.transpose(1, 2, 0).reshape(-1, req_dev),
        lengths.reshape(1, req_dev),
    )
    if far > 1:
        rows = lax.all_to_all(
            rows, "page", split_axis=0, concat_axis=0, axis_index_groups=far_groups, tiled=True
        )
    rows = rows.reshape(count, full)
    base = (lax.axis_index("page") // near * near).astype(jnp.int32).reshape(1)
    cell_rows, sel = pl.pallas_call(
        functools.partial(select_kernel, far, hops),
        out_shape=(
            jax.ShapeDtypeStruct((cells, full), BF16),
            jax.ShapeDtypeStruct((count, cells), F32),
        ),
        in_specs=[pl.BlockSpec(memory_space=pltpu.SMEM), vmem],
        out_specs=(vmem, vmem),
        compiler_params=params,
        name="select",
    )(base, rows)
    cell_rows = lax.all_to_all(
        cell_rows.reshape(near, far * SLOT, full), "page", split_axis=0, concat_axis=0,
        axis_index_groups=near_groups, tiled=True,
    ).reshape(cells, full)
    partial = pl.pallas_call(
        attend_kernel,
        out_shape=jax.ShapeDtypeStruct((cells, full), BF16),
        in_specs=[vmem] * 3,
        out_specs=vmem,
        scratch_shapes=[
            pltpu.VMEM((8, cells), jnp.int32),
            pltpu.SMEM((8, cells), jnp.int32),
            pltpu.VMEM((BLOCK * heads, HEAD), F32),
            pltpu.VMEM((cells * heads, HEAD), F32),
            pltpu.VMEM((cells * heads, HEAD), BF16),
            pltpu.VMEM((cells * heads, HEAD), F32),
            pltpu.VMEM((BLOCK * heads, HEAD), F32),
            pltpu.SemaphoreType.DMA,
        ],
        compiler_params=params,
        name="attend",
    )(cell_rows, cache_keys, cache_values)
    partial = lax.all_to_all(
        partial.reshape(near, far * SLOT, full), "page", split_axis=0, concat_axis=0,
        axis_index_groups=near_groups, tiled=True,
    ).reshape(cells, full)
    if far > 1:
        partial = pl.pallas_call(
            functools.partial(merge_kernel, False),
            out_shape=jax.ShapeDtypeStruct((count, full), BF16),
            in_specs=[vmem] * 2,
            out_specs=vmem,
            compiler_params=params,
            name="merge_near",
        )(partial, sel)
        partial = lax.all_to_all(
            partial.reshape(far, req_dev, full), "page", split_axis=0, concat_axis=0,
            axis_index_groups=far_groups, tiled=True,
        ).reshape(count, full)
        sel = (
            jnp.arange(count, dtype=jnp.int32)[None, :] % req_dev
            == jnp.arange(req_dev, dtype=jnp.int32)[:, None]
        ).astype(F32)
    return pl.pallas_call(
        functools.partial(merge_kernel, True),
        out_shape=jax.ShapeDtypeStruct((req_dev, width), BF16),
        in_specs=[vmem] * 2,
        out_specs=vmem,
        compiler_params=params,
        name="merge_far",
    )(partial, sel)


def solution(mesh):
    placed = (
        P("page", "mp"),
        P("page", None, "mp"),
        P("page", None, "mp"),
        P("page", None),
        P("page", None, None),
        P("page"),
    )
    return jax.shard_map(
        per_device, mesh=mesh, in_specs=placed, out_specs=P("page", "mp"), check_vma=False
    )
```

```python
import functools

import jax
import jax.numpy as jnp
from jax import lax
from jax.experimental import pallas as pl
from jax.experimental.pallas import tpu as pltpu
from jax.sharding import PartitionSpec as P

HEAD = 128
FAR = 8
PLANE = 8
SLOT = 2
BLOCK = 32
DEAD = -1e30
EXTRA = 128
F32 = jnp.float32
BF16 = jnp.bfloat16


def iota(shape, dim):
    return lax.broadcasted_iota(jnp.int32, shape, dim)


def pieces(x):
    high = x.astype(BF16).astype(F32)
    mid = (x - high).astype(BF16).astype(F32)
    low = (x - high - mid).astype(BF16).astype(F32)
    return high, mid, low


def pack_kernel(
    hop_tok, queries_in, routes_in, tables_in, lengths_in, out_ref,
    queries_ref, routes_ref, tables_ref, lengths_ref, sems,
):
    far, req_dev, width = out_ref.shape
    width -= EXTRA
    copies = [
        pltpu.make_async_copy(a, b, sems.at[n])
        for n, (a, b) in enumerate(
            [
                (queries_in, queries_ref),
                (routes_in, routes_ref),
                (tables_in, tables_ref),
                (lengths_in, lengths_ref),
            ]
        )
    ]
    for copy in copies:
        copy.start()
    for copy in copies:
        copy.wait()
    hops = routes_ref.shape[0]
    live = jnp.clip(lengths_ref[...] - iota((hops, req_dev), 0) * hop_tok, 0, hop_tok)
    told = jnp.concatenate([routes_ref[...], live, tables_ref[...]], axis=0).astype(F32)
    told = jnp.concatenate([told, jnp.zeros((told.shape[0], 128 - req_dev), F32)], axis=1)
    told = jnp.concatenate([told, jnp.zeros((EXTRA - told.shape[0], 128), F32)], axis=0)
    told = told.T[:req_dev].astype(BF16)
    for n in range(far):
        out_ref[n, :, :width] = queries_ref[...]
        out_ref[n, :, width:] = told


def select_kernel(far, hops, base_ref, rows_ref, out_ref, sel_ref):
    count, width = rows_ref.shape
    width -= EXTRA
    cells = out_ref.shape[0]
    req_dev = count // far
    info = rows_ref[:, width:].astype(F32)
    lane = iota((count, cells), 1)
    row = iota((count, cells), 0)
    dest = (lane // (SLOT * far) + base_ref[0]).astype(F32)
    own = (lane // SLOT) % far == row // req_dev
    named = jnp.zeros((count, cells), F32)
    first = jnp.zeros((count, cells), F32)
    second = jnp.zeros((count, cells), F32)
    live = jnp.zeros((count, cells), F32)
    for hop in range(hops):
        hit = (info[:, hop : hop + 1] == dest) & own
        named = jnp.where(hit, 1.0, named)
        live = jnp.where(hit, info[:, hops + hop : hops + hop + 1], live)
        at = 2 * hops + 2 * hop
        first = jnp.where(hit, info[:, at : at + 1], first)
        second = jnp.where(hit, info[:, at + 1 : at + 2], second)
    a = iota((count, count), 0)
    b = iota((count, count), 1)
    before = jnp.where((a // req_dev == b // req_dev) & (b < a), 1.0, 0.0).astype(BF16)
    rank = jnp.dot(before, named.astype(BF16), preferred_element_type=F32)
    sel = jnp.where(rank == (lane % SLOT).astype(F32), named, 0.0)
    sel_ref[...] = sel
    told = jnp.concatenate(
        [
            jnp.sum(sel * first, axis=0, keepdims=True),
            jnp.sum(sel * second, axis=0, keepdims=True),
            jnp.sum(sel * live, axis=0, keepdims=True),
            jnp.zeros((EXTRA - 3, cells), F32),
        ],
        axis=0,
    )
    out_ref[:, width:] = told.T.astype(BF16)
    place = sel.T.astype(BF16)
    step = 256
    for col in range(0, width, step):
        out_ref[:, col : col + step] = jnp.dot(
            place, rows_ref[:, col : col + step], preferred_element_type=F32
        ).astype(BF16)


def attend_kernel(
    rows_ref,
    keys_ref,
    values_ref,
    out_ref,
    told_ref,
    told_smem,
    query_ref,
    score_ref,
    prob_ref,
    inverse_ref,
    mixed_ref,
    sem,
):
    cells, width = rows_ref.shape
    width -= EXTRA
    heads = width // HEAD
    group = heads // 2
    hop_tok = 2 * keys_ref.shape[1]
    scale = HEAD ** -0.5
    told_ref[...] = rows_ref[:, width:].astype(F32).T[:8].astype(jnp.int32)
    copy = pltpu.make_async_copy(told_ref, told_smem, sem)
    copy.start()
    copy.wait()
    block = BLOCK
    blocks = cells // block
    tile = 16
    token = iota((heads, hop_tok), 1)
    lane = iota((heads, cells), 1)
    zero = jnp.zeros((group, HEAD), F32)

    def pages(ref, cell):
        return jnp.concatenate([ref[told_smem[which, cell]] for which in (0, 1)], axis=0)

    def scores(i):
        start = pl.multiple_of(i * block, block)
        for sub in range(0, block, tile):
            for head in range(heads):
                to = sub * heads + head * tile
                query_ref[to : to + tile, :] = rows_ref[
                    pl.ds(start + sub, tile), head * HEAD : (head + 1) * HEAD
                ].astype(F32)
        for cell in range(block):
            at = cell // tile * tile * heads + cell % tile
            query = query_ref[pl.ds(at, heads, stride=tile), :]
            spread = jnp.concatenate(
                [
                    jnp.concatenate([query[:group], zero], axis=1),
                    jnp.concatenate([zero, query[group:]], axis=1),
                ],
                axis=0,
            )
            at = pl.multiple_of((start + cell) * heads, heads)
            score_ref[pl.ds(at, heads), :] = lax.dot_general(
                spread.astype(BF16),
                pages(keys_ref, start + cell),
                (((1,), (1,)), ((), ())),
                preferred_element_type=F32,
            )

    def softmax(i, carries):
        start = pl.multiple_of(i * block, block)
        for cell in range(block):
            at = pl.multiple_of((start + cell) * heads, heads)
            own = score_ref[pl.ds(at, heads), :] * scale
            own = jnp.where(token < told_smem[2, start + cell], own, DEAD)
            top = jnp.max(own, axis=1, keepdims=True)
            probs = jnp.exp(own - top)
            total = jnp.sum(probs, axis=1, keepdims=True)
            carries = jnp.where(lane == start + cell, top + jnp.log(total), carries)
            prob_ref[pl.ds(at, heads), :] = probs.astype(BF16)
            inverse_ref[pl.ds(at, heads), :] = jnp.broadcast_to(1.0 / total, (heads, HEAD))
        return carries

    def mix(i):
        start = pl.multiple_of(i * block, block)
        for cell in range(block):
            at = pl.multiple_of((start + cell) * heads, heads)
            mixed = jnp.dot(
                prob_ref[pl.ds(at, heads), :],
                pages(values_ref, start + cell),
                preferred_element_type=F32,
            )
            inverse = inverse_ref[pl.ds(at, heads), :]
            to = cell * heads
            mixed_ref[to : to + group, :] = mixed[:group, :HEAD] * inverse[:group]
            mixed_ref[to + group : to + heads, :] = mixed[group:, HEAD:] * inverse[group:]
        for sub in range(0, block, tile):
            for head in range(heads):
                out_ref[pl.ds(start + sub, tile), head * HEAD : (head + 1) * HEAD] = mixed_ref[
                    pl.ds(sub * heads + head, tile, stride=heads), :
                ].astype(BF16)

    def step(i, carries):
        mix(i - 2)
        carries = softmax(i - 1, carries)
        scores(i)
        return carries

    scores(0)
    carries = softmax(0, jnp.zeros((heads, cells), F32))
    scores(1)
    carries = lax.fori_loop(2, blocks, step, carries)
    mix(blocks - 2)
    carries = softmax(blocks - 1, carries)
    mix(blocks - 1)
    told = jnp.concatenate(
        [*pieces(carries), jnp.zeros((EXTRA - 3 * heads, cells), F32)], axis=0
    )
    out_ref[:, width:] = told.T.astype(BF16)


def merge_kernel(last, rows_ref, sel_ref, out_ref):
    cells, width = rows_ref.shape
    width -= EXTRA
    heads = width // HEAD
    count = sel_ref.shape[0]
    chosen = sel_ref[...] > 0.0
    info = rows_ref[:, width:].astype(F32)
    if cells < 128:
        info = jnp.concatenate([info, jnp.zeros((128 - cells, EXTRA), F32)], axis=0)
    info = info.T
    carries = (info[:heads] + info[heads : 2 * heads] + info[2 * heads : 3 * heads])[:, :cells]
    lane = iota((count, EXTRA), 1)
    told = jnp.zeros((count, EXTRA), F32)
    some = jnp.max(sel_ref[...], axis=1, keepdims=True) > 0.0
    for head in range(heads):
        carry = jnp.broadcast_to(carries[head : head + 1], (count, cells))
        carry = jnp.where(chosen, carry, DEAD)
        high = jnp.max(carry, axis=1, keepdims=True)
        share = jnp.exp(carry - high)
        total = jnp.sum(share, axis=1, keepdims=True)
        share = share * (1.0 / total)
        major = share.astype(BF16)
        values = rows_ref[:, head * HEAD : (head + 1) * HEAD]
        if last:
            minor = (share - major.astype(F32)).astype(BF16)
            both = jnp.dot(
                jnp.concatenate([major, minor], axis=0), values, preferred_element_type=F32
            )
            merged = both[:count] + both[count:]
        else:
            merged = jnp.dot(major, values, preferred_element_type=F32)
            carry = jnp.where(some, high + jnp.log(total), DEAD)
            for n, part in enumerate(pieces(carry)):
                told = jnp.where(lane == n * heads + head, part, told)
        out_ref[:, head * HEAD : (head + 1) * HEAD] = merged.astype(BF16)
    if not last:
        out_ref[:, width:] = told.astype(BF16)


def far_sets(far, near):
    turn = [[m ^ PLANE if n >= far // 2 else m for m in range(near)] for n in range(far)]
    return [[n * near + turn[n][m] for n in range(far)] for m in range(near)]


def per_device(queries, cache_keys, cache_values, routes, page_table, lengths):
    pages = lax.axis_size("page")
    far, near = FAR, pages // FAR
    near_groups = [[n * near + m for m in range(near)] for n in range(far)]
    far_groups = far_sets(far, near)
    req_dev, hops = routes.shape
    width = queries.shape[1]
    heads = width // HEAD
    hop_tok = page_table.shape[2] * cache_keys.shape[1]
    cells = near * far * SLOT
    count = far * req_dev
    full = width + EXTRA
    vmem = pl.BlockSpec(memory_space=pltpu.VMEM)
    params = pltpu.CompilerParams(vmem_limit_bytes=48 * 1024 * 1024)

    rows = pl.pallas_call(
        functools.partial(pack_kernel, hop_tok),
        out_shape=jax.ShapeDtypeStruct((far, req_dev, full), BF16),
        in_specs=[pl.BlockSpec(memory_space=pl.ANY)] * 4,
        out_specs=vmem,
        scratch_shapes=[
            pltpu.VMEM((req_dev, width), BF16),
            pltpu.VMEM((hops, req_dev), jnp.int32),
            pltpu.VMEM((hops * page_table.shape[2], req_dev), jnp.int32),
            pltpu.VMEM((1, req_dev), jnp.int32),
            pltpu.SemaphoreType.DMA((4,)),
        ],
        compiler_params=pltpu.CompilerParams(vmem_limit_bytes=60 * 1024 * 1024),
        name="pack",
    )(
        queries,
        routes.T,
        page_table.transpose(1, 2, 0).reshape(-1, req_dev),
        lengths.reshape(1, req_dev),
    )
    if far > 1:
        rows = lax.all_to_all(
            rows, "page", split_axis=0, concat_axis=0, axis_index_groups=far_groups, tiled=True
        )
    rows = rows.reshape(count, full)
    base = (lax.axis_index("page") // near * near).astype(jnp.int32).reshape(1)
    cell_rows, sel = pl.pallas_call(
        functools.partial(select_kernel, far, hops),
        out_shape=(
            jax.ShapeDtypeStruct((cells, full), BF16),
            jax.ShapeDtypeStruct((count, cells), F32),
        ),
        in_specs=[pl.BlockSpec(memory_space=pltpu.SMEM), vmem],
        out_specs=(vmem, vmem),
        compiler_params=params,
        name="select",
    )(base, rows)
    cell_rows = lax.all_to_all(
        cell_rows.reshape(near, far * SLOT, full), "page", split_axis=0, concat_axis=0,
        axis_index_groups=near_groups, tiled=True,
    ).reshape(cells, full)
    partial = pl.pallas_call(
        attend_kernel,
        out_shape=jax.ShapeDtypeStruct((cells, full), BF16),
        in_specs=[vmem] * 3,
        out_specs=vmem,
        scratch_shapes=[
            pltpu.VMEM((8, cells), jnp.int32),
            pltpu.SMEM((8, cells), jnp.int32),
            pltpu.VMEM((BLOCK * heads, HEAD), F32),
            pltpu.VMEM((cells * heads, HEAD), F32),
            pltpu.VMEM((cells * heads, HEAD), BF16),
            pltpu.VMEM((cells * heads, HEAD), F32),
            pltpu.VMEM((BLOCK * heads, HEAD), F32),
            pltpu.SemaphoreType.DMA,
        ],
        compiler_params=params,
        name="attend",
    )(cell_rows, cache_keys, cache_values)
    partial = lax.all_to_all(
        partial.reshape(near, far * SLOT, full), "page", split_axis=0, concat_axis=0,
        axis_index_groups=near_groups, tiled=True,
    ).reshape(cells, full)
    if far > 1:
        partial = pl.pallas_call(
            functools.partial(merge_kernel, False),
            out_shape=jax.ShapeDtypeStruct((count, full), BF16),
            in_specs=[vmem] * 2,
            out_specs=vmem,
            compiler_params=params,
            name="merge_near",
        )(partial, sel)
        partial = lax.all_to_all(
            partial.reshape(far, req_dev, full), "page", split_axis=0, concat_axis=0,
            axis_index_groups=far_groups, tiled=True,
        ).reshape(count, full)
        sel = (
            jnp.arange(count, dtype=jnp.int32)[None, :] % req_dev
            == jnp.arange(req_dev, dtype=jnp.int32)[:, None]
        ).astype(F32)
    return pl.pallas_call(
        functools.partial(merge_kernel, True),
        out_shape=jax.ShapeDtypeStruct((req_dev, width), BF16),
        in_specs=[vmem] * 2,
        out_specs=vmem,
        compiler_params=params,
        name="merge_far",
    )(partial, sel)


def solution(mesh):
    placed = (
        P("page", "mp"),
        P("page", None, "mp"),
        P("page", None, "mp"),
        P("page", None),
        P("page", None, None),
        P("page"),
    )
    return jax.shard_map(
        per_device, mesh=mesh, in_specs=placed, out_specs=P("page", "mp"), check_vma=False
    )
```

```python
import functools

import jax
import jax.numpy as jnp
from jax import lax
from jax.experimental import pallas as pl
from jax.experimental.pallas import tpu as pltpu
from jax.sharding import PartitionSpec as P

HEAD = 128
LANES = 128
FAR = 8
PLANE = 8
SLOT = 2
TILE = 16
EXTRA = 8
BLOCK = 32
DEAD = -1e30
F32 = jnp.float32
BF16 = jnp.bfloat16


def iota(shape, dim):
    return lax.broadcasted_iota(jnp.int32, shape, dim)


def pieces(x):
    high = x.astype(BF16).astype(F32)
    mid = (x - high).astype(BF16).astype(F32)
    low = (x - high - mid).astype(BF16).astype(F32)
    return high, mid, low


def arrange(parts):
    lane = iota((EXTRA, LANES), 1) // TILE
    out = jnp.zeros((EXTRA, LANES), F32)
    for n, (x, group) in enumerate(parts):
        shift = (n - group) * TILE % LANES
        out = jnp.where(lane == n, pltpu.roll(x, shift, 1) if shift else x, out)
    return out


def extra_of(ref, n):
    return ref[n, ref.shape[1] - EXTRA :, :].astype(F32)


def put_extra(ref, n, x):
    ref[n, ref.shape[1] - EXTRA :, :] = x.astype(BF16)


def put_carries(ref, columns):
    wide = LANES // TILE
    for n in range(ref.shape[0]):
        at = n // wide * LANES
        put_extra(
            ref,
            n,
            arrange(
                [
                    (columns[v : v + EXTRA, at : at + LANES], n % wide)
                    for v in range(0, columns.shape[0], EXTRA)
                ]
            ),
        )


def get_carries(ref, heads):
    wide = LANES // TILE
    sums = []
    for n in range(ref.shape[0]):
        x = extra_of(ref, n)
        sums.append(
            x + pltpu.roll(x, LANES - heads // EXTRA * TILE, 1)
            + pltpu.roll(x, LANES - 2 * (heads // EXTRA) * TILE, 1)
        )
    return jnp.concatenate(
        [
            jnp.concatenate(
                [
                    arrange([(x, group) for x in sums[at : at + wide]])
                    for at in range(0, len(sums), wide)
                ],
                axis=1,
            )
            for group in range(heads // EXTRA)
        ],
        axis=0,
    )


def pack_kernel(
    hop_tok, queries_in, routes_in, tables_in, lengths_in, out_ref,
    queries_ref, routes_ref, tables_ref, lengths_ref, sems,
):
    far = out_ref.shape[0]
    hops, req_dev = routes_ref.shape
    copies = [
        pltpu.make_async_copy(a, b, sems.at[n])
        for n, (a, b) in enumerate(
            [
                (queries_in, queries_ref),
                (routes_in, routes_ref),
                (tables_in, tables_ref),
                (lengths_in, lengths_ref),
            ]
        )
    ]
    for copy in copies:
        copy.start()
    for copy in copies:
        copy.wait()
    live = jnp.clip(lengths_ref[...] - iota((hops, req_dev), 0) * hop_tok, 0, hop_tok)
    kinds = [
        routes_ref[...],
        live,
        tables_ref[pl.ds(0, hops, stride=2), :],
        tables_ref[pl.ds(1, hops, stride=2), :],
    ]
    blank = jnp.zeros((hops, LANES - req_dev), F32)
    told = arrange([(jnp.concatenate([x.astype(F32), blank], axis=1), 0) for x in kinds])
    for n in range(far):
        for head in range(queries_ref.shape[1] // HEAD):
            out_ref[n, head * TILE : (head + 1) * TILE, :] = queries_ref[
                :, head * HEAD : (head + 1) * HEAD
            ]
        put_extra(out_ref, n, told)


def select_kernel(base_ref, rows_ref, out_ref, sel_ref):
    far, near = rows_ref.shape[0], out_ref.shape[0]
    heads = (rows_ref.shape[1] - EXTRA) // TILE
    count, cells = far * TILE, near * TILE
    hops = EXTRA
    told = [extra_of(rows_ref, n) for n in range(far)]
    routes, live, first, second = [arrange([(x, kind) for x in told]) for kind in range(4)]
    coded = first + 32.0 * second + 1024.0 * live
    info = jnp.concatenate([routes, coded, jnp.zeros((LANES - 2 * hops, LANES), F32)], axis=0).T
    lane = iota((count, cells), 1)
    row = iota((count, cells), 0)
    dest = (lane // TILE + base_ref[0]).astype(F32)
    own = (lane // SLOT) % far == row // TILE
    named = jnp.zeros((count, cells), F32)
    code = jnp.zeros((count, cells), F32)
    for hop in range(hops):
        hit = (info[:, hop : hop + 1] == dest) & own
        named = jnp.where(hit, 1.0, named)
        code = jnp.where(hit, info[:, hops + hop : hops + hop + 1], code)
    a = iota((count, count), 0)
    b = iota((count, count), 1)
    before = jnp.where((a // TILE == b // TILE) & (b < a), 1.0, 0.0).astype(BF16)
    rank = jnp.dot(before, named.astype(BF16), preferred_element_type=F32)
    sel = jnp.where(rank == (lane % SLOT).astype(F32), named, 0.0)
    sel_ref[...] = sel
    code = jnp.sum(sel * code, axis=0, keepdims=True)
    live = jnp.floor(code * (1.0 / 1024.0))
    code = code - 1024.0 * live
    second = jnp.floor(code * (1.0 / 32.0))
    first = code - 32.0 * second
    told = jnp.concatenate([first, second, live, jnp.zeros((EXTRA - 3, cells), F32)], axis=0)
    wide = LANES // TILE
    for n in range(near):
        at = n // wide * LANES
        put_extra(out_ref, n, arrange([(told[:, at : at + LANES], n % wide)]))
    place = sel.T.astype(BF16)
    for head in range(0, heads, 2):
        at = head * TILE
        both = jnp.concatenate(
            [
                rows_ref[:, at : at + TILE, :].reshape(count, HEAD),
                rows_ref[:, at + TILE : at + 2 * TILE, :].reshape(count, HEAD),
            ],
            axis=1,
        )
        both = jnp.dot(place, both, preferred_element_type=F32).astype(BF16)
        out_ref[:, at : at + TILE, :] = both[:, :HEAD].reshape(near, TILE, HEAD)
        out_ref[:, at + TILE : at + 2 * TILE, :] = both[:, HEAD:].reshape(near, TILE, HEAD)


def attend_kernel(
    rows_ref,
    keys_ref,
    values_ref,
    out_ref,
    told_ref,
    told_smem,
    query_ref,
    score_ref,
    prob_ref,
    inverse_ref,
    mixed_ref,
    sem,
):
    near = rows_ref.shape[0]
    heads = (rows_ref.shape[1] - EXTRA) // TILE
    cells = near * TILE
    group = heads // 2
    hop_tok = 2 * keys_ref.shape[1]
    scale = HEAD ** -0.5
    wide = LANES // TILE
    for at in range(0, near, wide):
        told_ref[:, at * TILE : at * TILE + LANES] = arrange(
            [(extra_of(rows_ref, at + n), 0) for n in range(wide)]
        ).astype(jnp.int32)
    copy = pltpu.make_async_copy(told_ref, told_smem, sem)
    copy.start()
    copy.wait()
    block = BLOCK
    blocks = cells // block
    token = iota((heads, hop_tok), 1)
    lane = iota((heads, cells), 1)
    zero = jnp.zeros((group, HEAD), F32)

    def pages(ref, cell):
        return jnp.concatenate([ref[told_smem[which, cell]] for which in (0, 1)], axis=0)

    def scores(i):
        start = pl.multiple_of(i * block, block)
        for sub in range(0, block, TILE):
            query_ref[sub * heads : (sub + TILE) * heads, :] = rows_ref[
                i * (block // TILE) + sub // TILE, : heads * TILE, :
            ].astype(F32)
        for cell in range(block):
            at = cell // TILE * TILE * heads + cell % TILE
            query = query_ref[pl.ds(at, heads, stride=TILE), :]
            spread = jnp.concatenate(
                [
                    jnp.concatenate([query[:group], zero], axis=1),
                    jnp.concatenate([zero, query[group:]], axis=1),
                ],
                axis=0,
            )
            at = pl.multiple_of((start + cell) * heads, heads)
            score_ref[pl.ds(at, heads), :] = lax.dot_general(
                spread.astype(BF16),
                pages(keys_ref, start + cell),
                (((1,), (1,)), ((), ())),
                preferred_element_type=F32,
            )

    def softmax(i, carries):
        start = pl.multiple_of(i * block, block)
        for cell in range(block):
            at = pl.multiple_of((start + cell) * heads, heads)
            own = score_ref[pl.ds(at, heads), :] * scale
            own = jnp.where(token < told_smem[2, start + cell], own, DEAD)
            top = jnp.max(own, axis=1, keepdims=True)
            probs = jnp.exp(own - top)
            total = jnp.sum(probs, axis=1, keepdims=True)
            carries = jnp.where(lane == start + cell, top + jnp.log(total), carries)
            prob_ref[pl.ds(at, heads), :] = probs.astype(BF16)
            inverse_ref[pl.ds(at, heads), :] = jnp.broadcast_to(1.0 / total, (heads, HEAD))
        return carries

    def mix(i):
        start = pl.multiple_of(i * block, block)
        for cell in range(block):
            at = pl.multiple_of((start + cell) * heads, heads)
            mixed = jnp.dot(
                prob_ref[pl.ds(at, heads), :],
                pages(values_ref, start + cell),
                preferred_element_type=F32,
            )
            inverse = inverse_ref[pl.ds(at, heads), :]
            to = cell * heads
            mixed_ref[to : to + group, :] = mixed[:group, :HEAD] * inverse[:group]
            mixed_ref[to + group : to + heads, :] = mixed[group:, HEAD:] * inverse[group:]
        for sub in range(0, block, TILE):
            for head in range(heads):
                out_ref[
                    i * (block // TILE) + sub // TILE, head * TILE : (head + 1) * TILE, :
                ] = mixed_ref[pl.ds(sub * heads + head, TILE, stride=heads), :].astype(BF16)

    def step(i, carries):
        mix(i - 2)
        carries = softmax(i - 1, carries)
        scores(i)
        return carries

    scores(0)
    carries = softmax(0, jnp.zeros((heads, cells), F32))
    scores(1)
    carries = lax.fori_loop(2, blocks, step, carries)
    mix(blocks - 2)
    carries = softmax(blocks - 1, carries)
    mix(blocks - 1)
    put_carries(out_ref, jnp.concatenate(pieces(carries), axis=0))


def merge_kernel(last, rows_ref, sel_ref, out_ref):
    heads = (rows_ref.shape[1] - EXTRA) // TILE
    cells = rows_ref.shape[0] * TILE
    count = sel_ref.shape[0]
    chosen = sel_ref[...] > 0.0
    carries = get_carries(rows_ref, heads)
    lane = iota((count, LANES), 1)
    told = jnp.zeros((count, LANES), F32)
    some = jnp.max(sel_ref[...], axis=1, keepdims=True) > 0.0
    for head in range(heads):
        carry = jnp.broadcast_to(carries[head : head + 1], (count, cells))
        carry = jnp.where(chosen, carry, DEAD)
        high = jnp.max(carry, axis=1, keepdims=True)
        share = jnp.exp(carry - high)
        total = jnp.sum(share, axis=1, keepdims=True)
        share = share * (1.0 / total)
        major = share.astype(BF16)
        values = rows_ref[:, head * TILE : (head + 1) * TILE, :].reshape(cells, HEAD)
        if last:
            minor = (share - major.astype(F32)).astype(BF16)
            both = jnp.dot(
                jnp.concatenate([major, minor], axis=0), values, preferred_element_type=F32
            )
            merged = both[:count] + both[count:]
            out_ref[:, head * HEAD : (head + 1) * HEAD] = merged.astype(BF16)
        else:
            merged = jnp.dot(major, values, preferred_element_type=F32)
            out_ref[:, head * TILE : (head + 1) * TILE, :] = merged.astype(BF16).reshape(
                count // TILE, TILE, HEAD
            )
            carry = jnp.where(some, high + jnp.log(total), DEAD)
            for n, part in enumerate(pieces(carry)):
                told = jnp.where(lane == n * heads + head, part, told)
    if not last:
        put_carries(out_ref, told.T[: 3 * heads])


def far_sets(far, near):
    turn = [[m ^ PLANE if n >= far // 2 else m for m in range(near)] for n in range(far)]
    return [[n * near + turn[n][m] for n in range(far)] for m in range(near)]


def per_device(queries, cache_keys, cache_values, routes, page_table, lengths):
    pages = lax.axis_size("page")
    far, near = FAR, pages // FAR
    near_groups = [[n * near + m for m in range(near)] for n in range(far)]
    far_groups = far_sets(far, near)
    req_dev, hops = routes.shape
    width = queries.shape[1]
    heads = width // HEAD
    hop_tok = page_table.shape[2] * cache_keys.shape[1]
    cells = near * far * SLOT
    count = far * req_dev
    tall = heads * TILE + EXTRA
    vmem = pl.BlockSpec(memory_space=pltpu.VMEM)
    params = pltpu.CompilerParams(vmem_limit_bytes=48 * 1024 * 1024)

    def exchange(x, groups):
        return lax.all_to_all(
            x, "page", split_axis=0, concat_axis=0, axis_index_groups=groups, tiled=True
        )

    rows = pl.pallas_call(
        functools.partial(pack_kernel, hop_tok),
        out_shape=jax.ShapeDtypeStruct((far, tall, HEAD), BF16),
        in_specs=[pl.BlockSpec(memory_space=pl.ANY)] * 4,
        out_specs=vmem,
        scratch_shapes=[
            pltpu.VMEM((req_dev, width), BF16),
            pltpu.VMEM((hops, req_dev), jnp.int32),
            pltpu.VMEM((hops * page_table.shape[2], req_dev), jnp.int32),
            pltpu.VMEM((1, req_dev), jnp.int32),
            pltpu.SemaphoreType.DMA((4,)),
        ],
        compiler_params=pltpu.CompilerParams(vmem_limit_bytes=60 * 1024 * 1024),
        name="pack",
    )(
        queries,
        routes.T,
        page_table.transpose(1, 2, 0).reshape(-1, req_dev),
        lengths.reshape(1, req_dev),
    )
    rows = exchange(rows, far_groups)
    base = (lax.axis_index("page") // near * near).astype(jnp.int32).reshape(1)
    cell_rows, sel = pl.pallas_call(
        select_kernel,
        out_shape=(
            jax.ShapeDtypeStruct((near, tall, HEAD), BF16),
            jax.ShapeDtypeStruct((count, cells), F32),
        ),
        in_specs=[pl.BlockSpec(memory_space=pltpu.SMEM), vmem],
        out_specs=(vmem, vmem),
        compiler_params=params,
        name="select",
    )(base, rows)
    cell_rows = exchange(cell_rows, near_groups)
    partial = pl.pallas_call(
        attend_kernel,
        out_shape=jax.ShapeDtypeStruct((near, tall, HEAD), BF16),
        in_specs=[vmem] * 3,
        out_specs=vmem,
        scratch_shapes=[
            pltpu.VMEM((8, cells), jnp.int32),
            pltpu.SMEM((8, cells), jnp.int32),
            pltpu.VMEM((BLOCK * heads, HEAD), F32),
            pltpu.VMEM((cells * heads, HEAD), F32),
            pltpu.VMEM((cells * heads, HEAD), BF16),
            pltpu.VMEM((cells * heads, HEAD), F32),
            pltpu.VMEM((BLOCK * heads, HEAD), F32),
            pltpu.SemaphoreType.DMA,
        ],
        compiler_params=params,
        name="attend",
    )(cell_rows, cache_keys, cache_values)
    partial = exchange(partial, near_groups)
    partial = pl.pallas_call(
        functools.partial(merge_kernel, False),
        out_shape=jax.ShapeDtypeStruct((far, tall, HEAD), BF16),
        in_specs=[vmem] * 2,
        out_specs=vmem,
        compiler_params=params,
        name="merge_near",
    )(partial, sel)
    partial = exchange(partial, far_groups)
    mine = (
        jnp.arange(count, dtype=jnp.int32)[None, :] % req_dev
        == jnp.arange(req_dev, dtype=jnp.int32)[:, None]
    ).astype(F32)
    return pl.pallas_call(
        functools.partial(merge_kernel, True),
        out_shape=jax.ShapeDtypeStruct((req_dev, width), BF16),
        in_specs=[vmem] * 2,
        out_specs=vmem,
        compiler_params=params,
        name="merge_far",
    )(partial, mine)


def solution(mesh):
    placed = (
        P("page", "mp"),
        P("page", None, "mp"),
        P("page", None, "mp"),
        P("page", None),
        P("page", None, None),
        P("page"),
    )
    return jax.shard_map(
        per_device, mesh=mesh, in_specs=placed, out_specs=P("page", "mp"), check_vma=False
    )
```

```python
import functools

import jax
import jax.numpy as jnp
from jax import lax
from jax.experimental import pallas as pl
from jax.experimental.pallas import tpu as pltpu
from jax.sharding import PartitionSpec as P

HEAD = 128
LANES = 128
FAR = 8
SLOT = 2
TILE = 16
EXTRA = 8
BLOCK = 32
DEAD = -1e30
F32 = jnp.float32
BF16 = jnp.bfloat16


def iota(shape, dim):
    return lax.broadcasted_iota(jnp.int32, shape, dim)


def pieces(x):
    high = x.astype(BF16).astype(F32)
    mid = (x - high).astype(BF16).astype(F32)
    low = (x - high - mid).astype(BF16).astype(F32)
    return high, mid, low


def arrange(parts):
    lane = iota((EXTRA, LANES), 1) // TILE
    out = jnp.zeros((EXTRA, LANES), F32)
    for n, (x, group) in enumerate(parts):
        shift = (n - group) * TILE % LANES
        out = jnp.where(lane == n, pltpu.roll(x, shift, 1) if shift else x, out)
    return out


def extra_of(ref, n):
    return ref[n, ref.shape[1] - EXTRA :, :].astype(F32)


def put_extra(ref, n, x):
    ref[n, ref.shape[1] - EXTRA :, :] = x.astype(BF16)


def put_carries(ref, columns):
    wide = LANES // TILE
    for n in range(ref.shape[0]):
        at = n // wide * LANES
        put_extra(
            ref,
            n,
            arrange(
                [
                    (columns[v : v + EXTRA, at : at + LANES], n % wide)
                    for v in range(0, columns.shape[0], EXTRA)
                ]
            ),
        )


def get_carries(ref, heads):
    wide = LANES // TILE
    sums = []
    for n in range(ref.shape[0]):
        x = extra_of(ref, n)
        sums.append(
            x + pltpu.roll(x, LANES - heads // EXTRA * TILE, 1)
            + pltpu.roll(x, LANES - 2 * (heads // EXTRA) * TILE, 1)
        )
    return jnp.concatenate(
        [
            jnp.concatenate(
                [
                    arrange([(x, group) for x in sums[at : at + wide]])
                    for at in range(0, len(sums), wide)
                ],
                axis=1,
            )
            for group in range(heads // EXTRA)
        ],
        axis=0,
    )


def pack_kernel(
    hop_tok, queries_in, routes_in, tables_in, lengths_in, out_ref,
    queries_ref, routes_ref, tables_ref, lengths_ref, sems,
):
    hops, req_dev = routes_ref.shape
    copies = [
        pltpu.make_async_copy(a, b, sems.at[n])
        for n, (a, b) in enumerate(
            [
                (queries_in, queries_ref),
                (routes_in, routes_ref),
                (tables_in, tables_ref),
                (lengths_in, lengths_ref),
            ]
        )
    ]
    for copy in copies:
        copy.start()
    for copy in copies:
        copy.wait()
    live = jnp.clip(lengths_ref[...] - iota((hops, req_dev), 0) * hop_tok, 0, hop_tok)
    kinds = [
        routes_ref[...],
        live,
        tables_ref[pl.ds(0, hops, stride=2), :],
        tables_ref[pl.ds(1, hops, stride=2), :],
    ]
    blank = jnp.zeros((hops, LANES - req_dev), F32)
    told = arrange([(jnp.concatenate([x.astype(F32), blank], axis=1), 0) for x in kinds])
    for head in range(queries_ref.shape[1] // HEAD):
        out_ref[head * TILE : (head + 1) * TILE, :] = queries_ref[
            :, head * HEAD : (head + 1) * HEAD
        ]
    out_ref[out_ref.shape[0] - EXTRA :, :] = told.astype(BF16)


def select_kernel(base_ref, rows_ref, out_ref, sel_ref):
    far, near = rows_ref.shape[0], out_ref.shape[0]
    heads = (rows_ref.shape[1] - EXTRA) // TILE
    count, cells = far * TILE, near * TILE
    hops = EXTRA
    told = [extra_of(rows_ref, n) for n in range(far)]
    routes, live, first, second = [arrange([(x, kind) for x in told]) for kind in range(4)]
    coded = first + 32.0 * second + 1024.0 * live
    info = jnp.concatenate([routes, coded, jnp.zeros((LANES - 2 * hops, LANES), F32)], axis=0).T
    lane = iota((count, cells), 1)
    row = iota((count, cells), 0)
    dest = (lane // TILE + base_ref[0]).astype(F32)
    own = (lane // SLOT) % far == row // TILE
    named = jnp.zeros((count, cells), F32)
    code = jnp.zeros((count, cells), F32)
    for hop in range(hops):
        hit = (info[:, hop : hop + 1] == dest) & own
        named = jnp.where(hit, 1.0, named)
        code = jnp.where(hit, info[:, hops + hop : hops + hop + 1], code)
    a = iota((count, count), 0)
    b = iota((count, count), 1)
    before = jnp.where((a // TILE == b // TILE) & (b < a), 1.0, 0.0).astype(BF16)
    rank = jnp.dot(before, named.astype(BF16), preferred_element_type=F32)
    sel = jnp.where(rank == (lane % SLOT).astype(F32), named, 0.0)
    sel_ref[...] = sel
    code = jnp.sum(sel * code, axis=0, keepdims=True)
    live = jnp.floor(code * (1.0 / 1024.0))
    code = code - 1024.0 * live
    second = jnp.floor(code * (1.0 / 32.0))
    first = code - 32.0 * second
    told = jnp.concatenate([first, second, live, jnp.zeros((EXTRA - 3, cells), F32)], axis=0)
    wide = LANES // TILE
    for n in range(near):
        at = n // wide * LANES
        put_extra(out_ref, n, arrange([(told[:, at : at + LANES], n % wide)]))
    place = sel.T.astype(BF16)
    for head in range(0, heads, 2):
        at = head * TILE
        both = jnp.concatenate(
            [
                rows_ref[:, at : at + TILE, :].reshape(count, HEAD),
                rows_ref[:, at + TILE : at + 2 * TILE, :].reshape(count, HEAD),
            ],
            axis=1,
        )
        both = jnp.dot(place, both, preferred_element_type=F32).astype(BF16)
        out_ref[:, at : at + TILE, :] = both[:, :HEAD].reshape(near, TILE, HEAD)
        out_ref[:, at + TILE : at + 2 * TILE, :] = both[:, HEAD:].reshape(near, TILE, HEAD)


def attend_kernel(
    rows_ref,
    keys_ref,
    values_ref,
    out_ref,
    told_ref,
    told_smem,
    query_ref,
    score_ref,
    prob_ref,
    inverse_ref,
    mixed_ref,
    sem,
):
    near = rows_ref.shape[0]
    heads = (rows_ref.shape[1] - EXTRA) // TILE
    cells = near * TILE
    group = heads // 2
    hop_tok = 2 * keys_ref.shape[1]
    scale = HEAD ** -0.5
    wide = LANES // TILE
    for at in range(0, near, wide):
        told_ref[:, at * TILE : at * TILE + LANES] = arrange(
            [(extra_of(rows_ref, at + n), 0) for n in range(wide)]
        ).astype(jnp.int32)
    copy = pltpu.make_async_copy(told_ref, told_smem, sem)
    copy.start()
    copy.wait()
    block = BLOCK
    blocks = cells // block
    token = iota((heads, hop_tok), 1)
    lane = iota((heads, cells), 1)
    zero = jnp.zeros((group, HEAD), F32)

    def pages(ref, cell):
        return jnp.concatenate([ref[told_smem[which, cell]] for which in (0, 1)], axis=0)

    def scores(i):
        start = pl.multiple_of(i * block, block)
        for sub in range(0, block, TILE):
            query_ref[sub * heads : (sub + TILE) * heads, :] = rows_ref[
                i * (block // TILE) + sub // TILE, : heads * TILE, :
            ].astype(F32)
        for cell in range(block):
            at = cell // TILE * TILE * heads + cell % TILE
            query = query_ref[pl.ds(at, heads, stride=TILE), :]
            spread = jnp.concatenate(
                [
                    jnp.concatenate([query[:group], zero], axis=1),
                    jnp.concatenate([zero, query[group:]], axis=1),
                ],
                axis=0,
            )
            at = pl.multiple_of((start + cell) * heads, heads)
            score_ref[pl.ds(at, heads), :] = lax.dot_general(
                spread.astype(BF16),
                pages(keys_ref, start + cell),
                (((1,), (1,)), ((), ())),
                preferred_element_type=F32,
            )

    def softmax(i, carries):
        start = pl.multiple_of(i * block, block)
        for cell in range(block):
            at = pl.multiple_of((start + cell) * heads, heads)
            own = score_ref[pl.ds(at, heads), :] * scale
            own = jnp.where(token < told_smem[2, start + cell], own, DEAD)
            top = jnp.max(own, axis=1, keepdims=True)
            probs = jnp.exp(own - top)
            total = jnp.sum(probs, axis=1, keepdims=True)
            carries = jnp.where(lane == start + cell, top + jnp.log(total), carries)
            prob_ref[pl.ds(at, heads), :] = probs.astype(BF16)
            inverse_ref[pl.ds(at, heads), :] = jnp.broadcast_to(1.0 / total, (heads, HEAD))
        return carries

    def mix(i):
        start = pl.multiple_of(i * block, block)
        for cell in range(block):
            at = pl.multiple_of((start + cell) * heads, heads)
            mixed = jnp.dot(
                prob_ref[pl.ds(at, heads), :],
                pages(values_ref, start + cell),
                preferred_element_type=F32,
            )
            inverse = inverse_ref[pl.ds(at, heads), :]
            to = cell * heads
            mixed_ref[to : to + group, :] = mixed[:group, :HEAD] * inverse[:group]
            mixed_ref[to + group : to + heads, :] = mixed[group:, HEAD:] * inverse[group:]
        for sub in range(0, block, TILE):
            for head in range(heads):
                out_ref[
                    i * (block // TILE) + sub // TILE, head * TILE : (head + 1) * TILE, :
                ] = mixed_ref[pl.ds(sub * heads + head, TILE, stride=heads), :].astype(BF16)

    def step(i, carries):
        mix(i - 2)
        carries = softmax(i - 1, carries)
        scores(i)
        return carries

    scores(0)
    carries = softmax(0, jnp.zeros((heads, cells), F32))
    scores(1)
    carries = lax.fori_loop(2, blocks, step, carries)
    mix(blocks - 2)
    carries = softmax(blocks - 1, carries)
    mix(blocks - 1)
    put_carries(out_ref, jnp.concatenate(pieces(carries), axis=0))


def merge_kernel(last, rows_ref, sel_ref, out_ref):
    heads = (rows_ref.shape[1] - EXTRA) // TILE
    cells = rows_ref.shape[0] * TILE
    count = sel_ref.shape[0]
    chosen = sel_ref[...] > 0.0
    carries = get_carries(rows_ref, heads)
    lane = iota((count, LANES), 1)
    told = jnp.zeros((count, LANES), F32)
    some = jnp.max(sel_ref[...], axis=1, keepdims=True) > 0.0
    for head in range(heads):
        carry = jnp.broadcast_to(carries[head : head + 1], (count, cells))
        carry = jnp.where(chosen, carry, DEAD)
        high = jnp.max(carry, axis=1, keepdims=True)
        share = jnp.exp(carry - high)
        total = jnp.sum(share, axis=1, keepdims=True)
        share = share * (1.0 / total)
        major = share.astype(BF16)
        values = rows_ref[:, head * TILE : (head + 1) * TILE, :].reshape(cells, HEAD)
        if last:
            minor = (share - major.astype(F32)).astype(BF16)
            both = jnp.dot(
                jnp.concatenate([major, minor], axis=0), values, preferred_element_type=F32
            )
            merged = both[:count] + both[count:]
            out_ref[:, head * HEAD : (head + 1) * HEAD] = merged.astype(BF16)
        else:
            merged = jnp.dot(major, values, preferred_element_type=F32)
            out_ref[:, head * TILE : (head + 1) * TILE, :] = merged.astype(BF16).reshape(
                count // TILE, TILE, HEAD
            )
            carry = jnp.where(some, high + jnp.log(total), DEAD)
            for n, part in enumerate(pieces(carry)):
                told = jnp.where(lane == n * heads + head, part, told)
    if not last:
        put_carries(out_ref, told.T[: 3 * heads])


def per_device(queries, cache_keys, cache_values, routes, page_table, lengths):
    pages = lax.axis_size("page")
    far, near = FAR, pages // FAR
    near_groups = [[n * near + m for m in range(near)] for n in range(far)]
    far_groups = [[n * near + m for n in range(far)] for m in range(near)]
    req_dev, hops = routes.shape
    width = queries.shape[1]
    heads = width // HEAD
    hop_tok = page_table.shape[2] * cache_keys.shape[1]
    cells = near * far * SLOT
    count = far * req_dev
    tall = heads * TILE + EXTRA
    vmem = pl.BlockSpec(memory_space=pltpu.VMEM)
    params = pltpu.CompilerParams(vmem_limit_bytes=48 * 1024 * 1024)

    def exchange(x, groups):
        return lax.all_to_all(
            x, "page", split_axis=0, concat_axis=0, axis_index_groups=groups, tiled=True
        )

    rows = pl.pallas_call(
        functools.partial(pack_kernel, hop_tok),
        out_shape=jax.ShapeDtypeStruct((tall, HEAD), BF16),
        in_specs=[pl.BlockSpec(memory_space=pl.ANY)] * 4,
        out_specs=vmem,
        scratch_shapes=[
            pltpu.VMEM((req_dev, width), BF16),
            pltpu.VMEM((hops, req_dev), jnp.int32),
            pltpu.VMEM((hops * page_table.shape[2], req_dev), jnp.int32),
            pltpu.VMEM((1, req_dev), jnp.int32),
            pltpu.SemaphoreType.DMA((4,)),
        ],
        compiler_params=pltpu.CompilerParams(vmem_limit_bytes=60 * 1024 * 1024),
        name="pack",
    )(
        queries,
        routes.T,
        page_table.transpose(1, 2, 0).reshape(-1, req_dev),
        lengths.reshape(1, req_dev),
    )
    rows = lax.all_gather(rows, "page", axis_index_groups=far_groups)
    base = (lax.axis_index("page") // near * near).astype(jnp.int32).reshape(1)
    cell_rows, sel = pl.pallas_call(
        select_kernel,
        out_shape=(
            jax.ShapeDtypeStruct((near, tall, HEAD), BF16),
            jax.ShapeDtypeStruct((count, cells), F32),
        ),
        in_specs=[pl.BlockSpec(memory_space=pltpu.SMEM), vmem],
        out_specs=(vmem, vmem),
        compiler_params=params,
        name="select",
    )(base, rows)
    cell_rows = exchange(cell_rows, near_groups)
    partial = pl.pallas_call(
        attend_kernel,
        out_shape=jax.ShapeDtypeStruct((near, tall, HEAD), BF16),
        in_specs=[vmem] * 3,
        out_specs=vmem,
        scratch_shapes=[
            pltpu.VMEM((8, cells), jnp.int32),
            pltpu.SMEM((8, cells), jnp.int32),
            pltpu.VMEM((BLOCK * heads, HEAD), F32),
            pltpu.VMEM((cells * heads, HEAD), F32),
            pltpu.VMEM((cells * heads, HEAD), BF16),
            pltpu.VMEM((cells * heads, HEAD), F32),
            pltpu.VMEM((BLOCK * heads, HEAD), F32),
            pltpu.SemaphoreType.DMA,
        ],
        compiler_params=params,
        name="attend",
    )(cell_rows, cache_keys, cache_values)
    partial = exchange(partial, near_groups)
    partial = pl.pallas_call(
        functools.partial(merge_kernel, False),
        out_shape=jax.ShapeDtypeStruct((far, tall, HEAD), BF16),
        in_specs=[vmem] * 2,
        out_specs=vmem,
        compiler_params=params,
        name="merge_near",
    )(partial, sel)
    partial = exchange(partial, far_groups)
    mine = (
        jnp.arange(count, dtype=jnp.int32)[None, :] % req_dev
        == jnp.arange(req_dev, dtype=jnp.int32)[:, None]
    ).astype(F32)
    return pl.pallas_call(
        functools.partial(merge_kernel, True),
        out_shape=jax.ShapeDtypeStruct((req_dev, width), BF16),
        in_specs=[vmem] * 2,
        out_specs=vmem,
        compiler_params=params,
        name="merge_far",
    )(partial, mine)


def solution(mesh):
    placed = (
        P("page", "mp"),
        P("page", None, "mp"),
        P("page", None, "mp"),
        P("page", None),
        P("page", None, None),
        P("page"),
    )
    return jax.shard_map(
        per_device, mesh=mesh, in_specs=placed, out_specs=P("page", "mp"), check_vma=False
    )
```

```python
import functools

import jax
import jax.numpy as jnp
from jax import lax
from jax.experimental import pallas as pl
from jax.experimental.pallas import tpu as pltpu
from jax.sharding import PartitionSpec as P

HEAD = 128
LANES = 128
FAR = 8
SLOT = 2
TILE = 16
EXTRA = 8
BLOCK = 32
DEAD = -1e30
F32 = jnp.float32
BF16 = jnp.bfloat16


def iota(shape, dim):
    return lax.broadcasted_iota(jnp.int32, shape, dim)


def pieces(x):
    high = x.astype(BF16).astype(F32)
    mid = (x - high).astype(BF16).astype(F32)
    low = (x - high - mid).astype(BF16).astype(F32)
    return high, mid, low


def arrange(parts):
    lane = iota((EXTRA, LANES), 1) // TILE
    out = jnp.zeros((EXTRA, LANES), F32)
    for n, (x, group) in enumerate(parts):
        shift = (n - group) * TILE % LANES
        out = jnp.where(lane == n, pltpu.roll(x, shift, 1) if shift else x, out)
    return out


def extra_of(ref, n):
    return ref[n, ref.shape[1] - EXTRA :, :].astype(F32)


def put_extra(ref, n, x):
    ref[n, ref.shape[1] - EXTRA :, :] = x.astype(BF16)


def put_carries(ref, columns):
    wide = LANES // TILE
    for n in range(ref.shape[0]):
        at = n // wide * LANES
        put_extra(
            ref,
            n,
            arrange(
                [
                    (columns[v : v + EXTRA, at : at + LANES], n % wide)
                    for v in range(0, columns.shape[0], EXTRA)
                ]
            ),
        )


def get_carries(ref, heads):
    wide = LANES // TILE
    sums = []
    for n in range(ref.shape[0]):
        x = extra_of(ref, n)
        sums.append(
            x + pltpu.roll(x, LANES - heads // EXTRA * TILE, 1)
            + pltpu.roll(x, LANES - 2 * (heads // EXTRA) * TILE, 1)
        )
    return jnp.concatenate(
        [
            jnp.concatenate(
                [
                    arrange([(x, group) for x in sums[at : at + wide]])
                    for at in range(0, len(sums), wide)
                ],
                axis=1,
            )
            for group in range(heads // EXTRA)
        ],
        axis=0,
    )


def pack_kernel(
    hop_tok, queries_in, routes_in, tables_in, lengths_in, out_ref,
    queries_ref, routes_ref, tables_ref, lengths_ref, sems,
):
    hops, req_dev = routes_ref.shape
    copies = [
        pltpu.make_async_copy(a, b, sems.at[n])
        for n, (a, b) in enumerate(
            [
                (queries_in, queries_ref),
                (routes_in, routes_ref),
                (tables_in, tables_ref),
                (lengths_in, lengths_ref),
            ]
        )
    ]
    for copy in copies:
        copy.start()
    for copy in copies:
        copy.wait()
    live = jnp.clip(lengths_ref[...] - iota((hops, req_dev), 0) * hop_tok, 0, hop_tok)
    kinds = [
        routes_ref[...],
        live,
        tables_ref[pl.ds(0, hops, stride=2), :],
        tables_ref[pl.ds(1, hops, stride=2), :],
    ]
    blank = jnp.zeros((hops, LANES - req_dev), F32)
    told = arrange([(jnp.concatenate([x.astype(F32), blank], axis=1), 0) for x in kinds])
    for head in range(queries_ref.shape[1] // HEAD):
        out_ref[head * TILE : (head + 1) * TILE, :] = queries_ref[
            :, head * HEAD : (head + 1) * HEAD
        ]
    out_ref[out_ref.shape[0] - EXTRA :, :] = told.astype(BF16)


def select_kernel(base_ref, rows_ref, out_ref, sel_ref):
    far, near = rows_ref.shape[0], out_ref.shape[0]
    heads = (rows_ref.shape[1] - EXTRA) // TILE
    count, cells = far * TILE, near * TILE
    hops = EXTRA
    told = [extra_of(rows_ref, n) for n in range(far)]
    routes, live, first, second = [arrange([(x, kind) for x in told]) for kind in range(4)]
    coded = first + 32.0 * second + 1024.0 * live
    info = jnp.concatenate([routes, coded, jnp.zeros((LANES - 2 * hops, LANES), F32)], axis=0).T
    lane = iota((count, cells), 1)
    row = iota((count, cells), 0)
    dest = (lane // TILE + base_ref[0]).astype(F32)
    own = (lane // SLOT) % far == row // TILE
    named = jnp.zeros((count, cells), F32)
    code = jnp.zeros((count, cells), F32)
    for hop in range(hops):
        hit = (info[:, hop : hop + 1] == dest) & own
        named = jnp.where(hit, 1.0, named)
        code = jnp.where(hit, info[:, hops + hop : hops + hop + 1], code)
    a = iota((count, count), 0)
    b = iota((count, count), 1)
    before = jnp.where((a // TILE == b // TILE) & (b < a), 1.0, 0.0).astype(BF16)
    rank = jnp.dot(before, named.astype(BF16), preferred_element_type=F32)
    sel = jnp.where(rank == (lane % SLOT).astype(F32), named, 0.0)
    sel_ref[...] = sel
    code = jnp.sum(sel * code, axis=0, keepdims=True)
    live = jnp.floor(code * (1.0 / 1024.0))
    code = code - 1024.0 * live
    second = jnp.floor(code * (1.0 / 32.0))
    first = code - 32.0 * second
    told = jnp.concatenate([first, second, live, jnp.zeros((EXTRA - 3, cells), F32)], axis=0)
    wide = LANES // TILE
    for n in range(near):
        at = n // wide * LANES
        put_extra(out_ref, n, arrange([(told[:, at : at + LANES], n % wide)]))
    place = sel.T.astype(BF16)
    for head in range(0, heads, 2):
        at = head * TILE
        both = jnp.concatenate(
            [
                rows_ref[:, at : at + TILE, :].reshape(count, HEAD),
                rows_ref[:, at + TILE : at + 2 * TILE, :].reshape(count, HEAD),
            ],
            axis=1,
        )
        both = jnp.dot(place, both, preferred_element_type=F32).astype(BF16)
        out_ref[:, at : at + TILE, :] = both[:, :HEAD].reshape(near, TILE, HEAD)
        out_ref[:, at + TILE : at + 2 * TILE, :] = both[:, HEAD:].reshape(near, TILE, HEAD)


def attend_kernel(
    rows_ref,
    keys_ref,
    values_ref,
    out_ref,
    told_ref,
    told_smem,
    query_ref,
    score_ref,
    prob_ref,
    inverse_ref,
    mixed_ref,
    sem,
):
    near = rows_ref.shape[0]
    heads = (rows_ref.shape[1] - EXTRA) // TILE
    cells = near * TILE
    group = heads // 2
    hop_tok = 2 * keys_ref.shape[1]
    scale = HEAD ** -0.5
    wide = LANES // TILE
    for at in range(0, near, wide):
        told_ref[:, at * TILE : at * TILE + LANES] = arrange(
            [(extra_of(rows_ref, at + n), 0) for n in range(wide)]
        ).astype(jnp.int32)
    copy = pltpu.make_async_copy(told_ref, told_smem, sem)
    copy.start()
    copy.wait()
    block = BLOCK
    blocks = cells // block
    token = iota((heads, hop_tok), 1)
    lane = iota((heads, cells), 1)
    zero = jnp.zeros((group, HEAD), F32)

    def pages(ref, cell):
        return jnp.concatenate([ref[told_smem[which, cell]] for which in (0, 1)], axis=0)

    def scores(i):
        start = pl.multiple_of(i * block, block)
        for sub in range(0, block, TILE):
            query_ref[sub * heads : (sub + TILE) * heads, :] = rows_ref[
                i * (block // TILE) + sub // TILE, : heads * TILE, :
            ].astype(F32)
        for cell in range(block):
            at = cell // TILE * TILE * heads + cell % TILE
            query = query_ref[pl.ds(at, heads, stride=TILE), :]
            spread = jnp.concatenate(
                [
                    jnp.concatenate([query[:group], zero], axis=1),
                    jnp.concatenate([zero, query[group:]], axis=1),
                ],
                axis=0,
            )
            at = pl.multiple_of((start + cell) * heads, heads)
            score_ref[pl.ds(at, heads), :] = lax.dot_general(
                spread.astype(BF16),
                pages(keys_ref, start + cell),
                (((1,), (1,)), ((), ())),
                preferred_element_type=F32,
            )

    def softmax(i, carries):
        start = pl.multiple_of(i * block, block)
        for cell in range(block):
            at = pl.multiple_of((start + cell) * heads, heads)
            own = score_ref[pl.ds(at, heads), :] * scale
            own = jnp.where(token < told_smem[2, start + cell], own, DEAD)
            top = jnp.max(own, axis=1, keepdims=True)
            probs = jnp.exp(own - top)
            total = jnp.sum(probs, axis=1, keepdims=True)
            carries = jnp.where(lane == start + cell, top + jnp.log(total), carries)
            prob_ref[pl.ds(at, heads), :] = probs.astype(BF16)
            inverse_ref[pl.ds(at, heads), :] = jnp.broadcast_to(1.0 / total, (heads, HEAD))
        return carries

    def mix(i):
        start = pl.multiple_of(i * block, block)
        for cell in range(block):
            at = pl.multiple_of((start + cell) * heads, heads)
            mixed = jnp.dot(
                prob_ref[pl.ds(at, heads), :],
                pages(values_ref, start + cell),
                preferred_element_type=F32,
            )
            inverse = inverse_ref[pl.ds(at, heads), :]
            to = cell * heads
            mixed_ref[to : to + group, :] = mixed[:group, :HEAD] * inverse[:group]
            mixed_ref[to + group : to + heads, :] = mixed[group:, HEAD:] * inverse[group:]
        for sub in range(0, block, TILE):
            for head in range(heads):
                out_ref[
                    i * (block // TILE) + sub // TILE, head * TILE : (head + 1) * TILE, :
                ] = mixed_ref[pl.ds(sub * heads + head, TILE, stride=heads), :].astype(BF16)

    def step(i, carries):
        mix(i - 2)
        carries = softmax(i - 1, carries)
        scores(i)
        return carries

    scores(0)
    carries = softmax(0, jnp.zeros((heads, cells), F32))
    scores(1)
    carries = lax.fori_loop(2, blocks, step, carries)
    mix(blocks - 2)
    carries = softmax(blocks - 1, carries)
    mix(blocks - 1)
    put_carries(out_ref, jnp.concatenate(pieces(carries), axis=0))


def merge_kernel(last, rows_ref, *refs):
    out_ref = refs[-1]
    heads = (rows_ref.shape[1] - EXTRA) // TILE
    cells = rows_ref.shape[0] * TILE
    if last:
        count = out_ref.shape[0]
        chosen = iota((count, cells), 1) % TILE == iota((count, cells), 0)
    else:
        sel = refs[0][...]
        count = sel.shape[0]
        chosen = sel > 0.0
    carries = get_carries(rows_ref, heads)
    lane = iota((count, LANES), 1)
    highs = jnp.zeros((count, LANES), F32)
    totals = jnp.ones((count, LANES), F32)
    ones = jnp.ones((cells, HEAD), BF16)
    for head in range(heads):
        carry = jnp.broadcast_to(carries[head : head + 1], (count, cells))
        carry = jnp.where(chosen, carry, DEAD)
        high = jnp.max(carry, axis=1, keepdims=True)
        share = jnp.exp(carry - high)
        major = share.astype(BF16)
        values = rows_ref[:, head * TILE : (head + 1) * TILE, :].reshape(cells, HEAD)
        values = jnp.concatenate([values, ones], axis=1)
        if last:
            minor = (share - major.astype(F32)).astype(BF16)
            both = jnp.dot(
                jnp.concatenate([major, minor], axis=0), values, preferred_element_type=F32
            )
            both = both[:count] + both[count:]
            merged = both[:, :HEAD] / both[:, HEAD:]
            out_ref[:, head * HEAD : (head + 1) * HEAD] = merged.astype(BF16)
        else:
            both = jnp.dot(major, values, preferred_element_type=F32)
            merged = both[:, :HEAD] / both[:, HEAD:]
            out_ref[:, head * TILE : (head + 1) * TILE, :] = merged.astype(BF16).reshape(
                count // TILE, TILE, HEAD
            )
            highs = jnp.where(lane == head, high, highs)
            totals = jnp.where(lane == head, both[:, HEAD:], totals)
    if not last:
        some = jnp.max(sel, axis=1, keepdims=True) > 0.0
        carry = jnp.where(some, highs + jnp.log(totals), DEAD).T[:heads]
        put_carries(out_ref, jnp.concatenate(pieces(carry), axis=0))


def per_device(queries, cache_keys, cache_values, routes, page_table, lengths):
    pages = lax.axis_size("page")
    far, near = FAR, pages // FAR
    near_groups = [[n * near + m for m in range(near)] for n in range(far)]
    far_groups = [[n * near + m for n in range(far)] for m in range(near)]
    req_dev, hops = routes.shape
    width = queries.shape[1]
    heads = width // HEAD
    hop_tok = page_table.shape[2] * cache_keys.shape[1]
    cells = near * far * SLOT
    count = far * req_dev
    tall = heads * TILE + EXTRA
    vmem = pl.BlockSpec(memory_space=pltpu.VMEM)
    params = pltpu.CompilerParams(vmem_limit_bytes=48 * 1024 * 1024)

    def exchange(x, groups):
        return lax.all_to_all(
            x, "page", split_axis=0, concat_axis=0, axis_index_groups=groups, tiled=True
        )

    rows = pl.pallas_call(
        functools.partial(pack_kernel, hop_tok),
        out_shape=jax.ShapeDtypeStruct((tall, HEAD), BF16),
        in_specs=[pl.BlockSpec(memory_space=pl.ANY)] * 4,
        out_specs=vmem,
        scratch_shapes=[
            pltpu.VMEM((req_dev, width), BF16),
            pltpu.VMEM((hops, req_dev), jnp.int32),
            pltpu.VMEM((hops * page_table.shape[2], req_dev), jnp.int32),
            pltpu.VMEM((1, req_dev), jnp.int32),
            pltpu.SemaphoreType.DMA((4,)),
        ],
        compiler_params=pltpu.CompilerParams(vmem_limit_bytes=60 * 1024 * 1024),
        name="pack",
    )(
        queries,
        routes.T,
        page_table.transpose(1, 2, 0).reshape(-1, req_dev),
        lengths.reshape(1, req_dev),
    )
    rows = lax.all_gather(rows, "page", axis_index_groups=far_groups)
    base = (lax.axis_index("page") // near * near).astype(jnp.int32).reshape(1)
    cell_rows, sel = pl.pallas_call(
        select_kernel,
        out_shape=(
            jax.ShapeDtypeStruct((near, tall, HEAD), BF16),
            jax.ShapeDtypeStruct((count, cells), F32),
        ),
        in_specs=[pl.BlockSpec(memory_space=pltpu.SMEM), vmem],
        out_specs=(vmem, vmem),
        compiler_params=params,
        name="select",
    )(base, rows)
    cell_rows = exchange(cell_rows, near_groups)
    partial = pl.pallas_call(
        attend_kernel,
        out_shape=jax.ShapeDtypeStruct((near, tall, HEAD), BF16),
        in_specs=[vmem] * 3,
        out_specs=vmem,
        scratch_shapes=[
            pltpu.VMEM((8, cells), jnp.int32),
            pltpu.SMEM((8, cells), jnp.int32),
            pltpu.VMEM((BLOCK * heads, HEAD), F32),
            pltpu.VMEM((cells * heads, HEAD), F32),
            pltpu.VMEM((cells * heads, HEAD), BF16),
            pltpu.VMEM((cells * heads, HEAD), F32),
            pltpu.VMEM((BLOCK * heads, HEAD), F32),
            pltpu.SemaphoreType.DMA,
        ],
        compiler_params=params,
        name="attend",
    )(cell_rows, cache_keys, cache_values)
    partial = exchange(partial, near_groups)
    partial = pl.pallas_call(
        functools.partial(merge_kernel, False),
        out_shape=jax.ShapeDtypeStruct((far, tall, HEAD), BF16),
        in_specs=[vmem] * 2,
        out_specs=vmem,
        compiler_params=params,
        name="merge_near",
    )(partial, sel)
    partial = exchange(partial, far_groups)
    return pl.pallas_call(
        functools.partial(merge_kernel, True),
        out_shape=jax.ShapeDtypeStruct((req_dev, width), BF16),
        in_specs=[vmem],
        out_specs=vmem,
        compiler_params=params,
        name="merge_far",
    )(partial)


def solution(mesh):
    placed = (
        P("page", "mp"),
        P("page", None, "mp"),
        P("page", None, "mp"),
        P("page", None),
        P("page", None, None),
        P("page"),
    )
    return jax.shard_map(
        per_device, mesh=mesh, in_specs=placed, out_specs=P("page", "mp"), check_vma=False
    )
```

```python
import functools

import jax
import jax.numpy as jnp
from jax import lax
from jax.experimental import pallas as pl
from jax.experimental.pallas import tpu as pltpu
from jax.sharding import PartitionSpec as P

HEAD = 128
LANES = 128
FAR = 8
SLOT = 2
TILE = 16
EXTRA = 8
BLOCK = 64
DEAD = -1e30
F32 = jnp.float32
BF16 = jnp.bfloat16


def iota(shape, dim):
    return lax.broadcasted_iota(jnp.int32, shape, dim)


def pieces(x):
    high = x.astype(BF16).astype(F32)
    mid = (x - high).astype(BF16).astype(F32)
    low = (x - high - mid).astype(BF16).astype(F32)
    return high, mid, low


def arrange(parts):
    lane = iota((EXTRA, LANES), 1) // TILE
    out = jnp.zeros((EXTRA, LANES), F32)
    for n, (x, group) in enumerate(parts):
        shift = (n - group) * TILE % LANES
        out = jnp.where(lane == n, pltpu.roll(x, shift, 1) if shift else x, out)
    return out


def extra_of(ref, n):
    return ref[n, ref.shape[1] - EXTRA :, :].astype(F32)


def put_extra(ref, n, x):
    ref[n, ref.shape[1] - EXTRA :, :] = x.astype(BF16)


def put_carries(ref, columns):
    wide = LANES // TILE
    for n in range(ref.shape[0]):
        at = n // wide * LANES
        put_extra(
            ref,
            n,
            arrange(
                [
                    (columns[v : v + EXTRA, at : at + LANES], n % wide)
                    for v in range(0, columns.shape[0], EXTRA)
                ]
            ),
        )


def get_carries(ref, heads):
    wide = LANES // TILE
    sums = []
    for n in range(ref.shape[0]):
        x = extra_of(ref, n)
        sums.append(
            x + pltpu.roll(x, LANES - heads // EXTRA * TILE, 1)
            + pltpu.roll(x, LANES - 2 * (heads // EXTRA) * TILE, 1)
        )
    return jnp.concatenate(
        [
            jnp.concatenate(
                [
                    arrange([(x, group) for x in sums[at : at + wide]])
                    for at in range(0, len(sums), wide)
                ],
                axis=1,
            )
            for group in range(heads // EXTRA)
        ],
        axis=0,
    )


def pack_kernel(
    hop_tok, queries_in, routes_in, tables_in, lengths_in, out_ref,
    queries_ref, routes_ref, tables_ref, lengths_ref, sems,
):
    hops, req_dev = routes_ref.shape
    copies = [
        pltpu.make_async_copy(a, b, sems.at[n])
        for n, (a, b) in enumerate(
            [
                (queries_in, queries_ref),
                (routes_in, routes_ref),
                (tables_in, tables_ref),
                (lengths_in, lengths_ref),
            ]
        )
    ]
    for copy in copies:
        copy.start()
    for copy in copies:
        copy.wait()
    live = jnp.clip(lengths_ref[...] - iota((hops, req_dev), 0) * hop_tok, 0, hop_tok)
    kinds = [
        routes_ref[...],
        live,
        tables_ref[pl.ds(0, hops, stride=2), :],
        tables_ref[pl.ds(1, hops, stride=2), :],
    ]
    blank = jnp.zeros((hops, LANES - req_dev), F32)
    told = arrange([(jnp.concatenate([x.astype(F32), blank], axis=1), 0) for x in kinds])
    for head in range(queries_ref.shape[1] // HEAD):
        out_ref[head * TILE : (head + 1) * TILE, :] = queries_ref[
            :, head * HEAD : (head + 1) * HEAD
        ]
    out_ref[out_ref.shape[0] - EXTRA :, :] = told.astype(BF16)


def select_kernel(base_ref, rows_ref, out_ref, sel_ref):
    far, near = rows_ref.shape[0], out_ref.shape[0]
    heads = (rows_ref.shape[1] - EXTRA) // TILE
    count, cells = far * TILE, near * TILE
    hops = EXTRA
    told = [extra_of(rows_ref, n) for n in range(far)]
    routes, live, first, second = [arrange([(x, kind) for x in told]) for kind in range(4)]
    coded = first + 32.0 * second + 1024.0 * live
    info = jnp.concatenate([routes, coded, jnp.zeros((LANES - 2 * hops, LANES), F32)], axis=0).T
    lane = iota((count, cells), 1)
    row = iota((count, cells), 0)
    dest = (lane // TILE + base_ref[0]).astype(F32)
    own = (lane // SLOT) % far == row // TILE
    named = jnp.zeros((count, cells), F32)
    code = jnp.zeros((count, cells), F32)
    for hop in range(hops):
        hit = (info[:, hop : hop + 1] == dest) & own
        named = jnp.where(hit, 1.0, named)
        code = jnp.where(hit, info[:, hops + hop : hops + hop + 1], code)
    a = iota((count, count), 0)
    b = iota((count, count), 1)
    before = jnp.where((a // TILE == b // TILE) & (b < a), 1.0, 0.0).astype(BF16)
    rank = jnp.dot(before, named.astype(BF16), preferred_element_type=F32)
    sel = jnp.where(rank == (lane % SLOT).astype(F32), named, 0.0)
    sel_ref[...] = sel
    code = jnp.sum(sel * code, axis=0, keepdims=True)
    live = jnp.floor(code * (1.0 / 1024.0))
    code = code - 1024.0 * live
    second = jnp.floor(code * (1.0 / 32.0))
    first = code - 32.0 * second
    told = jnp.concatenate([first, second, live, jnp.zeros((EXTRA - 3, cells), F32)], axis=0)
    wide = LANES // TILE
    for n in range(near):
        at = n // wide * LANES
        put_extra(out_ref, n, arrange([(told[:, at : at + LANES], n % wide)]))
    place = sel.T.astype(BF16)
    for head in range(0, heads, 2):
        at = head * TILE
        both = jnp.concatenate(
            [
                rows_ref[:, at : at + TILE, :].reshape(count, HEAD),
                rows_ref[:, at + TILE : at + 2 * TILE, :].reshape(count, HEAD),
            ],
            axis=1,
        )
        both = jnp.dot(place, both, preferred_element_type=F32).astype(BF16)
        out_ref[:, at : at + TILE, :] = both[:, :HEAD].reshape(near, TILE, HEAD)
        out_ref[:, at + TILE : at + 2 * TILE, :] = both[:, HEAD:].reshape(near, TILE, HEAD)


def attend_kernel(
    rows_ref,
    keys_ref,
    values_ref,
    out_ref,
    told_ref,
    told_smem,
    query_ref,
    score_ref,
    prob_ref,
    inverse_ref,
    mixed_ref,
    sem,
):
    near = rows_ref.shape[0]
    heads = (rows_ref.shape[1] - EXTRA) // TILE
    cells = near * TILE
    group = heads // 2
    hop_tok = 2 * keys_ref.shape[1]
    scale = HEAD ** -0.5
    wide = LANES // TILE
    for at in range(0, near, wide):
        told_ref[:, at * TILE : at * TILE + LANES] = arrange(
            [(extra_of(rows_ref, at + n), 0) for n in range(wide)]
        ).astype(jnp.int32)
    copy = pltpu.make_async_copy(told_ref, told_smem, sem)
    copy.start()
    copy.wait()
    block = BLOCK
    blocks = cells // block
    token = iota((heads, hop_tok), 1)
    lane = iota((heads, cells), 1)
    zero = jnp.zeros((group, HEAD), F32)

    def pages(ref, cell):
        return jnp.concatenate([ref[told_smem[which, cell]] for which in (0, 1)], axis=0)

    def scores(i):
        start = i * block
        for sub in range(0, block, TILE):
            query_ref[sub * heads : (sub + TILE) * heads, :] = rows_ref[
                i * (block // TILE) + sub // TILE, : heads * TILE, :
            ].astype(F32)
        for cell in range(block):
            at = cell // TILE * TILE * heads + cell % TILE
            query = query_ref[pl.ds(at, heads, stride=TILE), :]
            spread = jnp.concatenate(
                [
                    jnp.concatenate([query[:group], zero], axis=1),
                    jnp.concatenate([zero, query[group:]], axis=1),
                ],
                axis=0,
            )
            at = (start + cell) * heads
            score_ref[pl.ds(at, heads), :] = lax.dot_general(
                spread.astype(BF16),
                pages(keys_ref, start + cell),
                (((1,), (1,)), ((), ())),
                preferred_element_type=F32,
            )

    def softmax(i, carries):
        start = i * block
        for cell in range(block):
            at = (start + cell) * heads
            own = score_ref[pl.ds(at, heads), :] * scale
            own = jnp.where(token < told_smem[2, start + cell], own, DEAD)
            top = jnp.max(own, axis=1, keepdims=True)
            probs = jnp.exp(own - top)
            total = jnp.sum(probs, axis=1, keepdims=True)
            carries = jnp.where(lane == start + cell, top + jnp.log(total), carries)
            prob_ref[pl.ds(at, heads), :] = probs.astype(BF16)
            inverse_ref[pl.ds(at, heads), :] = jnp.broadcast_to(1.0 / total, (heads, HEAD))
        return carries

    def mix(i):
        start = i * block
        for cell in range(block):
            at = (start + cell) * heads
            mixed = jnp.dot(
                prob_ref[pl.ds(at, heads), :],
                pages(values_ref, start + cell),
                preferred_element_type=F32,
            )
            inverse = inverse_ref[pl.ds(at, heads), :]
            to = cell * heads
            mixed_ref[to : to + group, :] = mixed[:group, :HEAD] * inverse[:group]
            mixed_ref[to + group : to + heads, :] = mixed[group:, HEAD:] * inverse[group:]
        for sub in range(0, block, TILE):
            for head in range(heads):
                out_ref[
                    i * (block // TILE) + sub // TILE, head * TILE : (head + 1) * TILE, :
                ] = mixed_ref[pl.ds(sub * heads + head, TILE, stride=heads), :].astype(BF16)

    carries = jnp.zeros((heads, cells), F32)
    for i in range(blocks + 2):
        if i >= 2:
            mix(i - 2)
        if 1 <= i <= blocks:
            carries = softmax(i - 1, carries)
        if i < blocks:
            scores(i)
    put_carries(out_ref, jnp.concatenate(pieces(carries), axis=0))


def merge_kernel(last, rows_ref, *refs):
    out_ref = refs[-1]
    heads = (rows_ref.shape[1] - EXTRA) // TILE
    cells = rows_ref.shape[0] * TILE
    if last:
        count = out_ref.shape[0]
        chosen = iota((count, cells), 1) % TILE == iota((count, cells), 0)
    else:
        sel = refs[0][...]
        count = sel.shape[0]
        chosen = sel > 0.0
    carries = get_carries(rows_ref, heads)
    lane = iota((count, LANES), 1)
    highs = jnp.zeros((count, LANES), F32)
    totals = jnp.ones((count, LANES), F32)
    ones = jnp.ones((cells, HEAD), BF16)
    for head in range(heads):
        carry = jnp.broadcast_to(carries[head : head + 1], (count, cells))
        carry = jnp.where(chosen, carry, DEAD)
        high = jnp.max(carry, axis=1, keepdims=True)
        share = jnp.exp(carry - high)
        major = share.astype(BF16)
        values = rows_ref[:, head * TILE : (head + 1) * TILE, :].reshape(cells, HEAD)
        values = jnp.concatenate([values, ones], axis=1)
        if last:
            minor = (share - major.astype(F32)).astype(BF16)
            both = jnp.dot(
                jnp.concatenate([major, minor], axis=0), values, preferred_element_type=F32
            )
            both = both[:count] + both[count:]
            merged = both[:, :HEAD] / both[:, HEAD:]
            out_ref[:, head * HEAD : (head + 1) * HEAD] = merged.astype(BF16)
        else:
            both = jnp.dot(major, values, preferred_element_type=F32)
            merged = both[:, :HEAD] / both[:, HEAD:]
            out_ref[:, head * TILE : (head + 1) * TILE, :] = merged.astype(BF16).reshape(
                count // TILE, TILE, HEAD
            )
            highs = jnp.where(lane == head, high, highs)
            totals = jnp.where(lane == head, both[:, HEAD:], totals)
    if not last:
        some = jnp.max(sel, axis=1, keepdims=True) > 0.0
        carry = jnp.where(some, highs + jnp.log(totals), DEAD).T[:heads]
        put_carries(out_ref, jnp.concatenate(pieces(carry), axis=0))


def per_device(queries, cache_keys, cache_values, routes, page_table, lengths):
    pages = lax.axis_size("page")
    far, near = FAR, pages // FAR
    near_groups = [[n * near + m for m in range(near)] for n in range(far)]
    far_groups = [[n * near + m for n in range(far)] for m in range(near)]
    req_dev, hops = routes.shape
    width = queries.shape[1]
    heads = width // HEAD
    hop_tok = page_table.shape[2] * cache_keys.shape[1]
    cells = near * far * SLOT
    count = far * req_dev
    tall = heads * TILE + EXTRA
    vmem = pl.BlockSpec(memory_space=pltpu.VMEM)
    params = pltpu.CompilerParams(vmem_limit_bytes=48 * 1024 * 1024)

    def exchange(x, groups):
        return lax.all_to_all(
            x, "page", split_axis=0, concat_axis=0, axis_index_groups=groups, tiled=True
        )

    rows = pl.pallas_call(
        functools.partial(pack_kernel, hop_tok),
        out_shape=jax.ShapeDtypeStruct((tall, HEAD), BF16),
        in_specs=[pl.BlockSpec(memory_space=pl.ANY)] * 4,
        out_specs=vmem,
        scratch_shapes=[
            pltpu.VMEM((req_dev, width), BF16),
            pltpu.VMEM((hops, req_dev), jnp.int32),
            pltpu.VMEM((hops * page_table.shape[2], req_dev), jnp.int32),
            pltpu.VMEM((1, req_dev), jnp.int32),
            pltpu.SemaphoreType.DMA((4,)),
        ],
        compiler_params=pltpu.CompilerParams(vmem_limit_bytes=60 * 1024 * 1024),
        name="pack",
    )(
        queries,
        routes.T,
        page_table.transpose(1, 2, 0).reshape(-1, req_dev),
        lengths.reshape(1, req_dev),
    )
    rows = lax.all_gather(rows, "page", axis_index_groups=far_groups)
    base = (lax.axis_index("page") // near * near).astype(jnp.int32).reshape(1)
    cell_rows, sel = pl.pallas_call(
        select_kernel,
        out_shape=(
            jax.ShapeDtypeStruct((near, tall, HEAD), BF16),
            jax.ShapeDtypeStruct((count, cells), F32),
        ),
        in_specs=[pl.BlockSpec(memory_space=pltpu.SMEM), vmem],
        out_specs=(vmem, vmem),
        compiler_params=params,
        name="select",
    )(base, rows)
    cell_rows = exchange(cell_rows, near_groups)
    partial = pl.pallas_call(
        attend_kernel,
        out_shape=jax.ShapeDtypeStruct((near, tall, HEAD), BF16),
        in_specs=[vmem] * 3,
        out_specs=vmem,
        scratch_shapes=[
            pltpu.VMEM((8, cells), jnp.int32),
            pltpu.SMEM((8, cells), jnp.int32),
            pltpu.VMEM((BLOCK * heads, HEAD), F32),
            pltpu.VMEM((cells * heads, HEAD), F32),
            pltpu.VMEM((cells * heads, HEAD), BF16),
            pltpu.VMEM((cells * heads, HEAD), F32),
            pltpu.VMEM((BLOCK * heads, HEAD), F32),
            pltpu.SemaphoreType.DMA,
        ],
        compiler_params=params,
        name="attend",
    )(cell_rows, cache_keys, cache_values)
    partial = exchange(partial, near_groups)
    partial = pl.pallas_call(
        functools.partial(merge_kernel, False),
        out_shape=jax.ShapeDtypeStruct((far, tall, HEAD), BF16),
        in_specs=[vmem] * 2,
        out_specs=vmem,
        compiler_params=params,
        name="merge_near",
    )(partial, sel)
    partial = exchange(partial, far_groups)
    return pl.pallas_call(
        functools.partial(merge_kernel, True),
        out_shape=jax.ShapeDtypeStruct((req_dev, width), BF16),
        in_specs=[vmem],
        out_specs=vmem,
        compiler_params=params,
        name="merge_far",
    )(partial)


def solution(mesh):
    placed = (
        P("page", "mp"),
        P("page", None, "mp"),
        P("page", None, "mp"),
        P("page", None),
        P("page", None, None),
        P("page"),
    )
    return jax.shard_map(
        per_device, mesh=mesh, in_specs=placed, out_specs=P("page", "mp"), check_vma=False
    )
```

```python
import functools

import jax
import jax.numpy as jnp
from jax import lax
from jax.experimental import pallas as pl
from jax.experimental.pallas import tpu as pltpu
from jax.sharding import PartitionSpec as P

HEAD = 128
LANES = 128
FAR = 8
SLOT = 2
TILE = 16
EXTRA = 8
BLOCK = 64
DEAD = -1e30
F32 = jnp.float32
BF16 = jnp.bfloat16


def iota(shape, dim):
    return lax.broadcasted_iota(jnp.int32, shape, dim)


def pieces(x):
    high = x.astype(BF16).astype(F32)
    mid = (x - high).astype(BF16).astype(F32)
    low = (x - high - mid).astype(BF16).astype(F32)
    return high, mid, low


def arrange(parts):
    lane = iota((EXTRA, LANES), 1) // TILE
    out = jnp.zeros((EXTRA, LANES), F32)
    for n, (x, group) in enumerate(parts):
        shift = (n - group) * TILE % LANES
        out = jnp.where(lane == n, pltpu.roll(x, shift, 1) if shift else x, out)
    return out


def extra_of(ref, n):
    return ref[n, ref.shape[1] - EXTRA :, :].astype(F32)


def put_extra(ref, n, x):
    ref[n, ref.shape[1] - EXTRA :, :] = x.astype(BF16)


def put_carries(ref, columns):
    wide = LANES // TILE
    for n in range(ref.shape[0]):
        at = n // wide * LANES
        put_extra(
            ref,
            n,
            arrange(
                [
                    (columns[v : v + EXTRA, at : at + LANES], n % wide)
                    for v in range(0, columns.shape[0], EXTRA)
                ]
            ),
        )


def get_carries(ref, heads):
    wide = LANES // TILE
    sums = []
    for n in range(ref.shape[0]):
        x = extra_of(ref, n)
        sums.append(
            x + pltpu.roll(x, LANES - heads // EXTRA * TILE, 1)
            + pltpu.roll(x, LANES - 2 * (heads // EXTRA) * TILE, 1)
        )
    return jnp.concatenate(
        [
            jnp.concatenate(
                [
                    arrange([(x, group) for x in sums[at : at + wide]])
                    for at in range(0, len(sums), wide)
                ],
                axis=1,
            )
            for group in range(heads // EXTRA)
        ],
        axis=0,
    )


def pack_kernel(
    hop_tok, queries_in, routes_in, tables_in, lengths_in, out_ref,
    queries_ref, routes_ref, tables_ref, lengths_ref, sems,
):
    hops, req_dev = routes_ref.shape
    copies = [
        pltpu.make_async_copy(a, b, sems.at[n])
        for n, (a, b) in enumerate(
            [
                (queries_in, queries_ref),
                (routes_in, routes_ref),
                (tables_in, tables_ref),
                (lengths_in, lengths_ref),
            ]
        )
    ]
    for copy in copies:
        copy.start()
    for copy in copies:
        copy.wait()
    live = jnp.clip(lengths_ref[...] - iota((hops, req_dev), 0) * hop_tok, 0, hop_tok)
    kinds = [
        routes_ref[...],
        live,
        tables_ref[pl.ds(0, hops, stride=2), :],
        tables_ref[pl.ds(1, hops, stride=2), :],
    ]
    blank = jnp.zeros((hops, LANES - req_dev), F32)
    told = arrange([(jnp.concatenate([x.astype(F32), blank], axis=1), 0) for x in kinds])
    for head in range(queries_ref.shape[1] // HEAD):
        out_ref[head * TILE : (head + 1) * TILE, :] = queries_ref[
            :, head * HEAD : (head + 1) * HEAD
        ]
    out_ref[out_ref.shape[0] - EXTRA :, :] = told.astype(BF16)


def select_kernel(base_ref, rows_ref, out_ref, sel_ref):
    far, near = rows_ref.shape[0], out_ref.shape[0]
    heads = (rows_ref.shape[1] - EXTRA) // TILE
    count, cells = far * TILE, near * TILE
    hops = EXTRA
    told = [extra_of(rows_ref, n) for n in range(far)]
    routes, live, first, second = [arrange([(x, kind) for x in told]) for kind in range(4)]
    coded = first + 32.0 * second + 1024.0 * live
    info = jnp.concatenate([routes, coded, jnp.zeros((LANES - 2 * hops, LANES), F32)], axis=0).T
    lane = iota((count, cells), 1)
    row = iota((count, cells), 0)
    dest = (lane // TILE + base_ref[0]).astype(F32)
    own = (lane // SLOT) % far == row // TILE
    named = jnp.zeros((count, cells), F32)
    code = jnp.zeros((count, cells), F32)
    for hop in range(hops):
        hit = (info[:, hop : hop + 1] == dest) & own
        named = jnp.where(hit, 1.0, named)
        code = jnp.where(hit, info[:, hops + hop : hops + hop + 1], code)
    a = iota((count, count), 0)
    b = iota((count, count), 1)
    before = jnp.where((a // TILE == b // TILE) & (b < a), 1.0, 0.0).astype(BF16)
    rank = jnp.dot(before, named.astype(BF16), preferred_element_type=F32)
    sel = jnp.where(rank == (lane % SLOT).astype(F32), named, 0.0)
    sel_ref[...] = sel.astype(BF16)
    code = jnp.sum(sel * code, axis=0, keepdims=True)
    live = jnp.floor(code * (1.0 / 1024.0))
    code = code - 1024.0 * live
    second = jnp.floor(code * (1.0 / 32.0))
    first = code - 32.0 * second
    told = jnp.concatenate([first, second, live, jnp.zeros((EXTRA - 3, cells), F32)], axis=0)
    wide = LANES // TILE
    for n in range(near):
        at = n // wide * LANES
        put_extra(out_ref, n, arrange([(told[:, at : at + LANES], n % wide)]))
    place = sel.T.astype(BF16)
    for head in range(0, heads, 2):
        at = head * TILE
        both = jnp.concatenate(
            [
                rows_ref[:, at : at + TILE, :].reshape(count, HEAD),
                rows_ref[:, at + TILE : at + 2 * TILE, :].reshape(count, HEAD),
            ],
            axis=1,
        )
        both = jnp.dot(place, both, preferred_element_type=F32).astype(BF16)
        out_ref[:, at : at + TILE, :] = both[:, :HEAD].reshape(near, TILE, HEAD)
        out_ref[:, at + TILE : at + 2 * TILE, :] = both[:, HEAD:].reshape(near, TILE, HEAD)


def attend_kernel(
    rows_ref,
    keys_ref,
    values_ref,
    out_ref,
    told_ref,
    told_smem,
    query_ref,
    score_ref,
    prob_ref,
    inverse_ref,
    mixed_ref,
    sem,
):
    near = rows_ref.shape[0]
    heads = (rows_ref.shape[1] - EXTRA) // TILE
    cells = near * TILE
    group = heads // 2
    hop_tok = 2 * keys_ref.shape[1]
    scale = HEAD ** -0.5
    wide = LANES // TILE
    for at in range(0, near, wide):
        told_ref[:, at * TILE : at * TILE + LANES] = arrange(
            [(extra_of(rows_ref, at + n), 0) for n in range(wide)]
        ).astype(jnp.int32)
    copy = pltpu.make_async_copy(told_ref, told_smem, sem)
    copy.start()
    copy.wait()
    block = BLOCK
    blocks = cells // block
    token = iota((heads, hop_tok), 1)
    lane = iota((heads, cells), 1)
    zero = jnp.zeros((group, HEAD), F32)

    def pages(ref, cell):
        return jnp.concatenate([ref[told_smem[which, cell]] for which in (0, 1)], axis=0)

    def scores(i):
        start = i * block
        for sub in range(0, block, TILE):
            query_ref[sub * heads : (sub + TILE) * heads, :] = rows_ref[
                i * (block // TILE) + sub // TILE, : heads * TILE, :
            ].astype(F32)
        for cell in range(block):
            at = cell // TILE * TILE * heads + cell % TILE
            query = query_ref[pl.ds(at, heads, stride=TILE), :]
            spread = jnp.concatenate(
                [
                    jnp.concatenate([query[:group], zero], axis=1),
                    jnp.concatenate([zero, query[group:]], axis=1),
                ],
                axis=0,
            )
            at = (start + cell) * heads
            score_ref[pl.ds(at, heads), :] = lax.dot_general(
                spread.astype(BF16),
                pages(keys_ref, start + cell),
                (((1,), (1,)), ((), ())),
                preferred_element_type=F32,
            )

    def softmax(i, carries):
        start = i * block
        for cell in range(block):
            at = (start + cell) * heads
            own = score_ref[pl.ds(at, heads), :] * scale
            own = jnp.where(token < told_smem[2, start + cell], own, DEAD)
            top = jnp.max(own, axis=1, keepdims=True)
            probs = jnp.exp(own - top)
            total = jnp.sum(probs, axis=1, keepdims=True)
            carries = jnp.where(lane == start + cell, top + jnp.log(total), carries)
            prob_ref[pl.ds(at, heads), :] = probs.astype(BF16)
            inverse_ref[pl.ds(at, heads), :] = jnp.broadcast_to(1.0 / total, (heads, HEAD))
        return carries

    def mix(i):
        start = i * block
        for cell in range(block):
            at = (start + cell) * heads
            mixed = jnp.dot(
                prob_ref[pl.ds(at, heads), :],
                pages(values_ref, start + cell),
                preferred_element_type=F32,
            )
            inverse = inverse_ref[pl.ds(at, heads), :]
            to = cell * heads
            mixed_ref[to : to + group, :] = mixed[:group, :HEAD] * inverse[:group]
            mixed_ref[to + group : to + heads, :] = mixed[group:, HEAD:] * inverse[group:]
        for sub in range(0, block, TILE):
            for head in range(heads):
                out_ref[
                    i * (block // TILE) + sub // TILE, head * TILE : (head + 1) * TILE, :
                ] = mixed_ref[pl.ds(sub * heads + head, TILE, stride=heads), :].astype(BF16)

    carries = jnp.zeros((heads, cells), F32)
    for i in range(blocks + 2):
        if i >= 2:
            mix(i - 2)
        if 1 <= i <= blocks:
            carries = softmax(i - 1, carries)
        if i < blocks:
            scores(i)
    put_carries(out_ref, jnp.concatenate(pieces(carries), axis=0))


def merge_kernel(last, rows_ref, *refs):
    out_ref = refs[-1]
    heads = (rows_ref.shape[1] - EXTRA) // TILE
    cells = rows_ref.shape[0] * TILE
    if last:
        count = out_ref.shape[0]
        chosen = iota((count, cells), 1) % TILE == iota((count, cells), 0)
    else:
        sel = refs[0][...].astype(F32)
        count = sel.shape[0]
        chosen = sel > 0.0
    carries = get_carries(rows_ref, heads)
    lane = iota((count, LANES), 1)
    highs = jnp.zeros((count, LANES), F32)
    totals = jnp.ones((count, LANES), F32)
    ones = jnp.ones((cells, HEAD), BF16)
    for head in range(heads):
        carry = jnp.broadcast_to(carries[head : head + 1], (count, cells))
        carry = jnp.where(chosen, carry, DEAD)
        high = jnp.max(carry, axis=1, keepdims=True)
        share = jnp.exp(carry - high)
        major = share.astype(BF16)
        values = rows_ref[:, head * TILE : (head + 1) * TILE, :].reshape(cells, HEAD)
        values = jnp.concatenate([values, ones], axis=1)
        if last:
            both = jnp.dot(major, values, preferred_element_type=F32)
            merged = both[:, :HEAD] / both[:, HEAD:]
            out_ref[:, head * HEAD : (head + 1) * HEAD] = merged.astype(BF16)
        else:
            both = jnp.dot(major, values, preferred_element_type=F32)
            merged = both[:, :HEAD] / both[:, HEAD:]
            out_ref[:, head * TILE : (head + 1) * TILE, :] = merged.astype(BF16).reshape(
                count // TILE, TILE, HEAD
            )
            highs = jnp.where(lane == head, high, highs)
            totals = jnp.where(lane == head, both[:, HEAD:], totals)
    if not last:
        some = jnp.max(sel, axis=1, keepdims=True) > 0.0
        carry = jnp.where(some, highs + jnp.log(totals), DEAD).T[:heads]
        put_carries(out_ref, jnp.concatenate(pieces(carry), axis=0))


def per_device(queries, cache_keys, cache_values, routes, page_table, lengths):
    pages = lax.axis_size("page")
    far, near = FAR, pages // FAR
    near_groups = [[n * near + m for m in range(near)] for n in range(far)]
    far_groups = [[n * near + m for n in range(far)] for m in range(near)]
    req_dev, hops = routes.shape
    width = queries.shape[1]
    heads = width // HEAD
    hop_tok = page_table.shape[2] * cache_keys.shape[1]
    cells = near * far * SLOT
    count = far * req_dev
    tall = heads * TILE + EXTRA
    vmem = pl.BlockSpec(memory_space=pltpu.VMEM)
    params = pltpu.CompilerParams(vmem_limit_bytes=48 * 1024 * 1024)

    def exchange(x, groups):
        return lax.all_to_all(
            x, "page", split_axis=0, concat_axis=0, axis_index_groups=groups, tiled=True
        )

    rows = pl.pallas_call(
        functools.partial(pack_kernel, hop_tok),
        out_shape=jax.ShapeDtypeStruct((tall, HEAD), BF16),
        in_specs=[pl.BlockSpec(memory_space=pl.ANY)] * 4,
        out_specs=vmem,
        scratch_shapes=[
            pltpu.VMEM((req_dev, width), BF16),
            pltpu.VMEM((hops, req_dev), jnp.int32),
            pltpu.VMEM((hops * page_table.shape[2], req_dev), jnp.int32),
            pltpu.VMEM((1, req_dev), jnp.int32),
            pltpu.SemaphoreType.DMA((4,)),
        ],
        compiler_params=pltpu.CompilerParams(vmem_limit_bytes=60 * 1024 * 1024),
        name="pack",
    )(
        queries,
        routes.T,
        page_table.transpose(1, 2, 0).reshape(-1, req_dev),
        lengths.reshape(1, req_dev),
    )
    rows = lax.all_gather(rows, "page", axis_index_groups=far_groups)
    base = (lax.axis_index("page") // near * near).astype(jnp.int32).reshape(1)
    cell_rows, sel = pl.pallas_call(
        select_kernel,
        out_shape=(
            jax.ShapeDtypeStruct((near, tall, HEAD), BF16),
            jax.ShapeDtypeStruct((count, cells), BF16),
        ),
        in_specs=[pl.BlockSpec(memory_space=pltpu.SMEM), vmem],
        out_specs=(vmem, vmem),
        compiler_params=params,
        name="select",
    )(base, rows)
    cell_rows = exchange(cell_rows, near_groups)
    partial = pl.pallas_call(
        attend_kernel,
        out_shape=jax.ShapeDtypeStruct((near, tall, HEAD), BF16),
        in_specs=[vmem] * 3,
        out_specs=vmem,
        scratch_shapes=[
            pltpu.VMEM((8, cells), jnp.int32),
            pltpu.SMEM((8, cells), jnp.int32),
            pltpu.VMEM((BLOCK * heads, HEAD), F32),
            pltpu.VMEM((cells * heads, HEAD), F32),
            pltpu.VMEM((cells * heads, HEAD), BF16),
            pltpu.VMEM((cells * heads, HEAD), F32),
            pltpu.VMEM((BLOCK * heads, HEAD), F32),
            pltpu.SemaphoreType.DMA,
        ],
        compiler_params=params,
        name="attend",
    )(cell_rows, cache_keys, cache_values)
    partial = exchange(partial, near_groups)
    partial = pl.pallas_call(
        functools.partial(merge_kernel, False),
        out_shape=jax.ShapeDtypeStruct((far, tall, HEAD), BF16),
        in_specs=[vmem] * 2,
        out_specs=vmem,
        compiler_params=params,
        name="merge_near",
    )(partial, sel)
    partial = exchange(partial, far_groups)
    return pl.pallas_call(
        functools.partial(merge_kernel, True),
        out_shape=jax.ShapeDtypeStruct((req_dev, width), BF16),
        in_specs=[vmem],
        out_specs=vmem,
        compiler_params=params,
        name="merge_far",
    )(partial)


def solution(mesh):
    placed = (
        P("page", "mp"),
        P("page", None, "mp"),
        P("page", None, "mp"),
        P("page", None),
        P("page", None, None),
        P("page"),
    )
    return jax.shard_map(
        per_device, mesh=mesh, in_specs=placed, out_specs=P("page", "mp"), check_vma=False
    )
```
